32 devices in a mesh: tp: 2 (over core), ep: 16 (over z, y, x).
Axes of the slice: x: 2, y: 2, z: 4, core: 2. Of those that a mesh axis runs over, the one named last changes fastest.
Arguments:
- hidden_in: bfloat16 [2048, 7168], P('ep', 'tp'), may hold values from -6 to 6
- query: bfloat16 [2048, 2048], P('ep', 'tp'), may hold values from -6 to 6
- key_in: bfloat16 [2048, 2048], P('ep', 'tp'), may hold values from -6 to 6
- value_in: bfloat16 [2048, 2048], P('ep', 'tp'), may hold values from -6 to 6
- out_weight: bfloat16 [2048, 7168], P(None, ('tp', 'ep')), may hold values from -0.125 to 0.125
- norm_gain: bfloat16 [7168], P('tp'), may hold values from 0.5 to 1.5
- router: bfloat16 [7168, 16], P('tp'), may hold values from -0.0625 to 0.0625
- routes: int32 [2048, 8], P('ep'), may hold values from 0 to 15, all different within a row; in each aligned block of 128 rows (0 to 127, 128 to 255, ...) at most 80 rows name the same one
- w_gate: bfloat16 [16, 7168, 1024], P('ep', 'tp'), may hold values from -0.0625 to 0.0625
- w_up: bfloat16 [16, 7168, 1024], P('ep', 'tp'), may hold values from -0.0625 to 0.0625
- w_down: bfloat16 [16, 1024, 7168], P('ep', None, 'tp'), may hold values from -0.1875 to 0.1875
- grad_out: bfloat16 [2048, 7168], P('ep', 'tp'), may hold values from -6 to 6
Outputs:
- grad_in: bfloat16 [2048, 7168], P('ep', 'tp')
- grad_query: bfloat16 [2048, 2048], P('ep', 'tp')
- grad_key: bfloat16 [2048, 2048], P('ep', 'tp')
- grad_value: bfloat16 [2048, 2048], P('ep', 'tp')
The draws below stay inside these ranges and needn't reach their ends.
Inputs may be any that keep to these rules, and one draw needn't show every extreme that they name: `routes`: each row names 8 different experts. Among the 128 rows of one sequence at most 80 name the same expert, and in every draw some expert is named by exactly 80 rows of some sequence.
All inputs are finite; a program needn't handle non-finite values.
Results may differ from the reference program's by a relative error of at most 0.025.
Values may be sent and summed in bfloat16 or wider, within the bound.
No kernel may reach another device: no remote copies, remote signals or barrier semaphores. Data moves between devices by JAX's collectives and lax.ppermute only.
A program may use at most 192 MiB of HBM per device.

```python
import math
import jax
import jax.numpy as jnp
import numpy as np
from jax import lax

D = 7168
HDIM = 128
EH = 1024
TOP = 8
SEQ = 128
EXPERTS = 16
HEADS = 16
CAP = 80
TOKENS = 2048
N_TP = 2
N_EP = 16


def draw_query(key, part):
    own_key = jax.random.fold_in(key, 1)
    drawn = jnp.clip(jax.random.normal(own_key, (TOKENS, HEADS * HDIM)), -6.0, 6.0)
    return drawn.astype(jnp.bfloat16)


def draw_key_in(key, part):
    own_key = jax.random.fold_in(key, 2)
    drawn = jnp.clip(jax.random.normal(own_key, (TOKENS, HEADS * HDIM)), -6.0, 6.0)
    return drawn.astype(jnp.bfloat16)


def block_scale(stream_key, extent, cuts, low, high):
    def one(position, parts):
        heights = jax.random.uniform(jax.random.fold_in(jax.random.fold_in(stream_key, 6), position), (parts,), jnp.float32, low / len(cuts), high / len(cuts))
        return jnp.repeat(jnp.exp(heights), extent[position] // parts).reshape((-1,) + (1,) * (len(extent) - position - 1))

    gain = one(*cuts[0])
    for cut in cuts[1:]:
        gain = gain * one(*cut)
    return gain


def assign_block(rng, own, number, rows, amount, top, most, skew):
    ranking = jax.random.permutation(rng, amount)
    packed, ordinary = portions_of(amount, rows * top, most, skew, True), portions_of(amount, rows * top, most, skew, False)
    places = jnp.arange(amount)

    def named(lengths, rotation):
        used = int((lengths > 0).sum())
        fixed = max(1, used // 4)
        moved = fixed + (places - fixed + rotation * (used - fixed)) % max(1, amount - fixed)
        return jnp.zeros((amount,), jnp.int32).at[ranking[jnp.where(places < fixed, places, moved)]].set(jnp.asarray(lengths, jnp.int32))

    lengths = jnp.where(number % 4 == 0, named(packed, number // 4), named(ordinary, number - number // 4 - 1))
    mixed = jax.random.permutation(jax.random.fold_in(own, 3), amount)
    donor, taker = mixed[0:amount // 2 * 2:2], mixed[1:amount // 2 * 2:2]
    room = jnp.minimum(lengths[donor] - 1, most - lengths[taker]) // 2
    room = jnp.where((donor == ranking[0]) | (taker == ranking[0]) | (lengths[taker] == 0), 0, jnp.maximum(room, 0))
    moved = jax.random.randint(jax.random.fold_in(own, 4), (amount // 2,), 0, 1 << 20) % (room + 1)
    lengths = lengths.at[donor].add(-moved).at[taker].add(moved)
    items = jnp.searchsorted(jnp.cumsum(lengths), jnp.arange(rows * top), side="right").astype(jnp.int32)
    grid = items.reshape(top, rows).T
    grid = grid[jax.random.permutation(jax.random.fold_in(own, 1), rows)]
    rotation = jax.random.randint(jax.random.fold_in(own, 2), (rows, 1), 0, top)
    return jnp.take_along_axis(grid, (jnp.arange(top)[None, :] + rotation) % top, axis=1)


def portions_of(count, total, reach, skew, full):
    portions = [(1 << 20) // math.isqrt(standing ** skew) + 1 for standing in range(1, count + 1)]
    largest = reach if full else min(reach, max(-(-total // count), total * portions[0] // sum(portions)))
    least = 1 if total - largest >= count - 1 else 0
    holding, surplus = [largest] + [least] * (count - 1), total - largest - least * (count - 1)
    while surplus > 0:
        candidates = [i for i in range(1, count) if holding[i] < largest] or [i for i in range(1, count) if holding[i] < reach]
        pool, budget = sum([portions[i] for i in candidates]), surplus
        for i in candidates:
            addition = min(reach - holding[i], max(1, budget * portions[i] // pool), surplus)
            holding[i] = holding[i] + addition
            surplus = surplus - addition
    return np.array(holding)


def normal_values(rng, dims, deviation, most, shards=(), kind=jnp.bfloat16):
    result = deviation * jax.random.normal(rng, dims, jnp.float32)
    if shards:
        result = result * block_scale(rng, dims, shards, -0.22, 0.18)
    return jnp.clip(result, -most, most).astype(kind)


def setup_inputs(seed: int = 0) -> dict:
    key_of = jax.random.split(jax.random.key(seed), 13)
    hidden_in = normal_values(key_of[0], (TOKENS, D), 1.0, 6.0, ((0, 16), (1, 2)))
    query = draw_query(jax.random.fold_in(key_of[12], 71), 0)
    key_in = draw_key_in(jax.random.fold_in(key_of[12], 71), 0)
    value_in = normal_values(key_of[3], (TOKENS, HEADS * HDIM), 1.0, 6.0, ((0, 16), (1, 2)))
    out_weight = normal_values(key_of[4], (HEADS * HDIM, D), (HEADS * HDIM) ** -0.5, 0.125, ((1, 32),))
    norm_gain = jnp.clip(1.0 + 0.1 * jax.random.normal(key_of[5], (D,), jnp.float32), 0.5, 1.5).astype(jnp.bfloat16)
    router = normal_values(key_of[6], (D, EXPERTS), D ** -0.5, 0.0625, ((0, 2),))
    routes_keys = jax.random.split(jax.random.fold_in(key_of[7], 1), TOKENS // SEQ)
    routes_turns = jax.random.permutation(jax.random.fold_in(key_of[7], 3), TOKENS // SEQ)
    routes = jax.vmap(lambda own, number: assign_block(jax.random.fold_in(key_of[7], 2), own, number, SEQ, EXPERTS, TOP, CAP, 2))(routes_keys, routes_turns).reshape((TOKENS, TOP))
    w_gate = normal_values(key_of[8], (EXPERTS, D, EH), D ** -0.5, 0.0625, ((0, 16), (1, 2)))
    w_up = normal_values(key_of[9], (EXPERTS, D, EH), D ** -0.5, 0.0625, ((0, 16), (1, 2)))
    w_down = normal_values(key_of[10], (EXPERTS, EH, D), EH ** -0.5, 0.1875, ((0, 16), (2, 2)))
    grad_out = normal_values(key_of[11], (TOKENS, D), 1.0, 6.0, ((0, 16), (1, 2)))
    return {"hidden_in": hidden_in, "query": query, "key_in": key_in, "value_in": value_in, "out_weight": out_weight, "norm_gain": norm_gain, "router": router, "routes": routes, "w_gate": w_gate, "w_up": w_up, "w_down": w_down, "grad_out": grad_out}


route_scale = 2.5
norm_eps = 1e-06
masked_score = -1e+30

def barrier_round(values):
    return lax.optimization_barrier(values.astype(jnp.bfloat16)).astype(jnp.float32)

def softmax_rows(query, key_in):
    length = query.shape[0]
    query_f = query.reshape(length, HEADS, HDIM).astype(jnp.float32)
    key_f = key_in.reshape(length, HEADS, HDIM).astype(jnp.float32)
    scores = jnp.einsum('qhd,khd->hqk', query_f, key_f) * (1.0 / math.sqrt(HDIM))
    causal = jnp.arange(length)[None, :] <= jnp.arange(length)[:, None]
    scores = jnp.where(causal[None], scores, masked_score)
    highest = lax.optimization_barrier(jnp.max(scores, axis=2, keepdims=True))
    weights_exp = jnp.exp(scores - highest)
    return weights_exp / lax.optimization_barrier(jnp.sum(weights_exp, axis=2, keepdims=True))

def attend_forward(block):
    query, key_in, value_in = block
    length = query.shape[0]
    prob_rounded = barrier_round(softmax_rows(query, key_in))
    value_f = value_in.reshape(length, HEADS, HDIM).astype(jnp.float32)
    attended = jnp.einsum('hqk,khd->qhd', prob_rounded, value_f)
    return attended.reshape(length, HEADS * HDIM).astype(jnp.bfloat16)

def attend_backward(block):
    query, key_in, value_in, grad_attn = block
    length = query.shape[0]
    probabilities = softmax_rows(query, key_in)
    prob_rounded = barrier_round(probabilities)
    query_f = query.reshape(length, HEADS, HDIM).astype(jnp.float32)
    key_f = key_in.reshape(length, HEADS, HDIM).astype(jnp.float32)
    value_f = value_in.reshape(length, HEADS, HDIM).astype(jnp.float32)
    grad_f = grad_attn.reshape(length, HEADS, HDIM).astype(jnp.float32)
    grad_value = jnp.einsum('hqk,qhd->khd', prob_rounded, grad_f)
    grad_prob = jnp.einsum('qhd,khd->hqk', grad_f, value_f)
    centre = lax.optimization_barrier(jnp.sum(probabilities * grad_prob, axis=2, keepdims=True))
    grad_score = barrier_round(probabilities * (grad_prob - centre))
    grad_query = jnp.einsum('hqk,khd->qhd', grad_score, key_f) * (1.0 / math.sqrt(HDIM))
    grad_key = jnp.einsum('hqk,qhd->khd', grad_score, query_f) * (1.0 / math.sqrt(HDIM))
    width = HEADS * HDIM
    return (grad_query.reshape(length, width).astype(jnp.bfloat16), grad_key.reshape(length, width).astype(jnp.bfloat16), grad_value.reshape(length, width).astype(jnp.bfloat16))

def sliced_product(row_block, weight):
    row_count = row_block.shape[0]
    rows_f = row_block.reshape(row_count, N_TP, -1).astype(jnp.float32)
    weight_f = weight.reshape(N_TP, -1, weight.shape[1]).astype(jnp.float32)
    partials = jnp.einsum('rtd,tdh->trh', rows_f, weight_f)
    return lax.optimization_barrier(jnp.sum(barrier_round(partials), axis=0))

def reference(hidden_in, query, key_in, value_in, out_weight, norm_gain, router, routes, w_gate, w_up, w_down, grad_out):
    width = HEADS * HDIM
    query_seq = query.reshape(N_EP, SEQ, width)
    key_seq = key_in.reshape(N_EP, SEQ, width)
    value_seq = value_in.reshape(N_EP, SEQ, width)
    attended = lax.map(attend_forward, (query_seq, key_seq, value_seq)).reshape(TOKENS, width)
    proj = jnp.dot(attended, out_weight, preferred_element_type=jnp.float32)
    residual = (hidden_in.astype(jnp.float32) + proj).astype(jnp.bfloat16)
    resid_f = residual.astype(jnp.float32)
    gain_f = norm_gain.astype(jnp.float32)
    router_f = router.astype(jnp.float32)
    inv_rms = lax.rsqrt(lax.optimization_barrier(jnp.mean(resid_f * resid_f, axis=1, keepdims=True)) + norm_eps)
    normed_f = resid_f * gain_f * inv_rms
    normed = normed_f.astype(jnp.bfloat16)
    logits = jnp.dot(normed_f, router_f, precision=lax.Precision.HIGHEST)
    expert_ids = jnp.arange(EXPERTS, dtype=jnp.int32)
    one_hot = routes[:, :, None] == expert_ids[None, None, :]
    sigmoids = jax.nn.sigmoid(logits)
    picked = lax.optimization_barrier(jnp.sum(jnp.where(one_hot, sigmoids[:, None, :], 0.0), axis=2))
    totals = lax.optimization_barrier(jnp.sum(picked, axis=1, keepdims=True))
    weights = route_scale * picked / totals
    flat_routes = routes.reshape(N_EP, SEQ * TOP)
    hot_int = (flat_routes[:, :, None] == expert_ids[None, None, :]).astype(jnp.int32)
    earlier = (jnp.cumsum(hot_int, axis=1) - hot_int).astype(jnp.int32)
    slots = lax.optimization_barrier(jnp.sum(earlier * hot_int, axis=2)).astype(jnp.int32)
    sequence_ids = jnp.arange(N_EP, dtype=jnp.int32)[:, None]
    destination = (flat_routes * (N_EP * CAP) + sequence_ids * CAP + slots).reshape(-1).astype(jnp.int32)
    row_numbers = jnp.arange(TOKENS * TOP, dtype=jnp.int32)
    table = jnp.full((EXPERTS * N_EP * CAP,), TOKENS * TOP, jnp.int32).at[destination].set(row_numbers)
    table = table.reshape(EXPERTS, N_EP * CAP)
    normed_pad = jnp.concatenate([normed, jnp.zeros((1, D), jnp.bfloat16)], axis=0)
    grad_pad = jnp.concatenate([grad_out, jnp.zeros((1, D), jnp.bfloat16)], axis=0)
    weight_pad = jnp.concatenate([weights.reshape(-1), jnp.zeros((1,), jnp.float32)], axis=0)

    def expert_step(carry, inputs):
        grad_acc, score_acc = carry
        row_ids, gate_weight, up_weight, down_weight = inputs
        token_ids = (row_ids // TOP).astype(jnp.int32)
        routed_in = normed_pad[token_ids]
        routed_grad = grad_pad[token_ids]
        gate_pre = sliced_product(routed_in, gate_weight)
        up_pre = sliced_product(routed_in, up_weight)
        back_pre = sliced_product(routed_grad, down_weight.T)
        gate_sigmoid = jax.nn.sigmoid(gate_pre)
        gate_silu = gate_pre * gate_sigmoid
        hidden_b = barrier_round(gate_silu * up_pre)
        score_b = barrier_round(lax.optimization_barrier(jnp.sum(hidden_b * back_pre, axis=1)))
        grad_gate = (back_pre * up_pre * gate_sigmoid * (1.0 + gate_pre * (1.0 - gate_sigmoid))).astype(jnp.bfloat16)
        grad_up = (back_pre * gate_silu).astype(jnp.bfloat16)
        expert_grad = barrier_round(jnp.dot(grad_gate, gate_weight.T, preferred_element_type=jnp.float32) + jnp.dot(grad_up, up_weight.T, preferred_element_type=jnp.float32))
        grad_acc = grad_acc.at[token_ids].add(weight_pad[row_ids][:, None] * expert_grad)
        score_acc = score_acc.at[row_ids].set(score_b)
        return ((grad_acc, score_acc), None)
    start_carry = (jnp.zeros((TOKENS + 1, D), jnp.float32), jnp.zeros((TOKENS * TOP + 1,), jnp.float32))
    (grad_acc, score_acc), unused = lax.scan(expert_step, start_carry, (table, w_gate, w_up, w_down))
    dnormed = grad_acc[:TOKENS]
    dweight = score_acc[:TOKENS * TOP].reshape(TOKENS, TOP)
    dpicked = route_scale / totals * (dweight - lax.optimization_barrier(jnp.sum(dweight * picked, axis=1, keepdims=True)) / totals)
    dlogits = lax.optimization_barrier(jnp.sum(jnp.where(one_hot, (dpicked * picked * (1.0 - picked))[:, :, None], 0.0), axis=1))
    dnorm_f = dnormed + jnp.dot(dlogits, router_f.T, precision=lax.Precision.HIGHEST)
    gained = gain_f * dnorm_f
    inner_sum = lax.optimization_barrier(jnp.sum(gained * resid_f, axis=1, keepdims=True))
    dresid = inv_rms * gained - resid_f * (inv_rms * inv_rms * inv_rms) * inner_sum / D
    grad_in = (grad_out.astype(jnp.float32) + dresid).astype(jnp.bfloat16)
    grad_attn = jnp.dot(grad_in, out_weight.T, preferred_element_type=jnp.float32).astype(jnp.bfloat16)
    grad_seq = grad_attn.reshape(N_EP, SEQ, width)
    grad_query, grad_key, grad_value = lax.map(attend_backward, (query_seq, key_seq, value_seq, grad_seq))
    return (grad_in, grad_query.reshape(TOKENS, width), grad_key.reshape(TOKENS, width), grad_value.reshape(TOKENS, width))
```

```python
import math

import jax
import jax.numpy as jnp
from jax import lax
from jax.sharding import PartitionSpec as P

D = 7168
HDIM = 128
TOP = 8
DEPTH = 4


route_scale = 2.5
norm_eps = 1e-06
masked_score = -1e30


def split_heads(values):
    return values.reshape(values.shape[0], values.shape[1] // HDIM, HDIM)


def softmax_rows(query_h, key_h):
    length = query_h.shape[0]
    scores = jnp.einsum("qhd,khd->hqk", query_h, key_h, preferred_element_type=jnp.float32) * (
        1.0 / math.sqrt(HDIM)
    )
    causal = jnp.arange(length)[None, :] <= jnp.arange(length)[:, None]
    scores = jnp.where(causal[None], scores, masked_score)
    highest = jnp.max(scores, axis=2, keepdims=True)
    weights_exp = jnp.exp(scores - highest)
    return weights_exp / jnp.sum(weights_exp, axis=2, keepdims=True)


def depth_permute(x, pairs, n_ep):
    plane = n_ep // DEPTH
    return lax.ppermute(
        x, "ep", [(a * plane + i, b * plane + i) for a, b in pairs for i in range(plane)]
    )


def plane_permute(x, step, n_ep):
    return lax.ppermute(x, "ep", [(i, i ^ step) for i in range(n_ep)])


SWAP = [(0, 1), (1, 0), (2, 3), (3, 2)]
MIDDLE = [(1, 2), (2, 1)]
OUTWARD = [(1, 0), (2, 3)]
INWARD = [(0, 1), (3, 2)]


def spread_depth(x, n_ep):
    partner = depth_permute(x, SWAP, n_ep)
    near = depth_permute(x, MIDDLE, n_ep)
    near = (near, depth_permute(near, OUTWARD, n_ep))
    far = depth_permute(partner, MIDDLE, n_ep)
    far = (far, depth_permute(far, OUTWARD, n_ep))
    return [x, partner, near[0] + near[1], far[0] + far[1]]


def depth_sources(z):
    return [z, z ^ 1, jnp.where(z < 2, 2, 1), jnp.where(z < 2, 3, 0)]


def exchange_plane(blocks, n_ep):
    parts = [blocks[0]]
    for step in range(1, blocks.shape[0]):
        parts.append(plane_permute(blocks[step], step, n_ep))
    return jnp.concatenate(parts, axis=0)


def tp_swap(x):
    return lax.ppermute(x, "tp", [(0, 1), (1, 0)])


def tp_sum(x):
    if lax.axis_size("tp") != 2:
        return lax.psum(x, "tp")
    return x + tp_swap(x)


def tp_reduce(x, axis):
    n_tp = lax.axis_size("tp")
    if n_tp != 2:
        return lax.psum_scatter(x, "tp", scatter_dimension=axis, tiled=True).astype(jnp.float32)
    t = lax.axis_index("tp")
    width = x.shape[axis] // 2
    mine = lax.dynamic_slice_in_dim(x, t * width, width, axis)
    other = lax.dynamic_slice_in_dim(x, (1 - t) * width, width, axis)
    return mine.astype(jnp.float32) + tp_swap(other).astype(jnp.float32)


def tp_gather(x, axis):
    n_tp = lax.axis_size("tp")
    if n_tp != 2:
        return lax.all_gather(x, "tp", axis=axis, tiled=True)
    t = lax.axis_index("tp")
    other = tp_swap(x)
    first = jnp.where(t == 0, x, other)
    second = jnp.where(t == 0, other, x)
    return jnp.concatenate([first, second], axis=axis)


def one_hot_slots(mask, capacity):
    length = mask.shape[-1]
    before = (jnp.arange(length)[:, None] < jnp.arange(length)[None, :]).astype(jnp.bfloat16)
    slots = jnp.einsum(
        "...i,ij->...j", mask.astype(jnp.bfloat16), before, preferred_element_type=jnp.float32
    )
    wanted = jnp.arange(capacity, dtype=jnp.float32)[:, None]
    return (mask[..., None, :] & (slots[..., None, :] == wanted)).astype(jnp.bfloat16)


def on_device(
    hidden_in,
    query,
    key_in,
    value_in,
    out_weight,
    norm_gain,
    router,
    routes,
    w_gate,
    w_up,
    w_down,
    grad_out,
):
    n_ep = lax.axis_size("ep")
    plane = n_ep // DEPTH
    me = lax.axis_index("ep")
    z, place = me // plane, me % plane
    length = hidden_in.shape[0]
    slice_width = hidden_in.shape[1]
    capacity = min(length, (5 * length * TOP + 4 * n_ep - 1) // (4 * n_ep))
    bf16 = jnp.bfloat16

    slab = lax.all_gather(out_weight, "ep", axis=1, tiled=True)

    routes_all = lax.all_gather(routes, "ep", axis=0)
    sources = jnp.stack(depth_sources(z))
    steps = jnp.arange(plane, dtype=jnp.int32)
    relay_seq = sources * plane + place
    relay_expert = z * plane + (place ^ steps)
    relay_mask = jnp.any(
        routes_all[relay_seq][:, None] == relay_expert[None, :, None, None], axis=-1
    )
    relay_hot = one_hot_slots(relay_mask, capacity).reshape(DEPTH, plane * capacity, length)
    expert_seq = sources[:, None] * plane + (place ^ steps)[None, :]
    expert_mask = jnp.any(routes_all[expert_seq] == me, axis=-1)
    expert_hot = one_hot_slots(expert_mask, capacity).astype(jnp.float32)

    def dispatch(x):
        rows = []
        for hot, piece in zip(relay_hot, spread_depth(x, n_ep)):
            packed = jnp.dot(hot, piece, preferred_element_type=jnp.float32).astype(bf16)
            rows.append(exchange_plane(packed.reshape(plane, capacity, slice_width), n_ep))
        return rows

    query_h = split_heads(query)
    key_h = split_heads(key_in)
    value_h = split_heads(value_in)
    probabilities = softmax_rows(query_h, key_h)
    prob_rounded = probabilities.astype(bf16)
    attended = jnp.einsum("hqk,khd->qhd", prob_rounded, value_h, preferred_element_type=jnp.float32)
    attended = attended.reshape(length, -1).astype(bf16)
    all_heads = tp_gather(attended, 1)

    grad_rows = dispatch(grad_out)

    proj = jnp.dot(all_heads, slab, preferred_element_type=jnp.float32)
    residual = (hidden_in.astype(jnp.float32) + proj).astype(bf16)
    resid_f = residual.astype(jnp.float32)
    gain_f = norm_gain.astype(jnp.float32)
    router_f = router.astype(jnp.float32)
    scaled = resid_f * gain_f
    squares = tp_sum(jnp.sum(resid_f * resid_f, axis=1))
    raw_logits = tp_sum(jnp.dot(scaled, router_f, precision=lax.Precision.HIGHEST))
    inv_rms = lax.rsqrt(squares[:, None] / D + norm_eps)
    normed = (scaled * inv_rms).astype(bf16)
    normed_rows = dispatch(normed)

    logits = raw_logits * inv_rms
    expert_ids = jnp.arange(n_ep, dtype=jnp.int32)
    one_hot = routes[:, :, None] == expert_ids[None, None, :]
    sigmoids = jax.nn.sigmoid(logits)
    picked = jnp.sum(jnp.where(one_hot, sigmoids[:, None, :], 0.0), axis=2)
    totals = jnp.sum(picked, axis=1, keepdims=True)
    weights = route_scale * picked / totals
    weight_table = jnp.sum(jnp.where(one_hot, weights[:, :, None], 0.0), axis=1)
    own_weights = lax.all_to_all(
        weight_table.T.reshape(n_ep, 1, length), "ep", split_axis=0, concat_axis=0, tiled=True
    ).reshape(n_ep, length)
    row_weights = jnp.sum(expert_hot * own_weights[expert_seq][:, :, None, :], axis=-1)
    row_weights = row_weights.reshape(DEPTH, plane * capacity, 1)

    gate_local = w_gate[0]
    up_local = w_up[0]
    down_local = w_down[0]
    row_count = plane * capacity
    back_pre = tp_reduce(
        jnp.einsum(
            "rd,hd->rh",
            jnp.concatenate(grad_rows, axis=0),
            down_local,
            preferred_element_type=jnp.float32,
        ).astype(bf16),
        1,
    )
    scores, sums = [None] * DEPTH, [None] * DEPTH
    for i in range(DEPTH):
        rows = normed_rows[i]
        gate_part = jnp.dot(rows, gate_local, preferred_element_type=jnp.float32).astype(bf16)
        up_part = jnp.dot(rows, up_local, preferred_element_type=jnp.float32).astype(bf16)
        pre_sums = tp_reduce(jnp.stack([gate_part, up_part]), 2)
        gate_pre, up_pre = pre_sums[0], pre_sums[1]
        back = back_pre[i * row_count : (i + 1) * row_count]
        gate_sigmoid = jax.nn.sigmoid(gate_pre)
        gate_silu = gate_pre * gate_sigmoid
        hidden_b = lax.optimization_barrier((gate_silu * up_pre).astype(bf16)).astype(jnp.float32)
        scores[i] = jnp.sum(hidden_b * back, axis=1)
        grad_gate = (back * up_pre * gate_sigmoid * (1.0 + gate_pre * (1.0 - gate_sigmoid))).astype(
            bf16
        )
        grad_up = (back * gate_silu).astype(bf16)
        both = tp_gather(jnp.stack([grad_gate, grad_up]), 2)
        expert_grad = jnp.einsum(
            "rh,dh->rd", both[0], gate_local, preferred_element_type=jnp.float32
        ) + jnp.einsum("rh,dh->rd", both[1], up_local, preferred_element_type=jnp.float32)
        back_rows = (expert_grad * row_weights[i]).astype(bf16)
        arrived = exchange_plane(back_rows.reshape(plane, capacity, slice_width), n_ep)
        sums[i] = jnp.einsum("ri,rd->id", relay_hot[i], arrived, preferred_element_type=jnp.float32)
    far = sums[3].astype(bf16)
    far = (sums[3] + depth_permute(far, INWARD, n_ep)).astype(bf16)
    near = sums[2].astype(bf16)
    near = (sums[2] + depth_permute(near, INWARD, n_ep)).astype(bf16)
    partner = (sums[1] + depth_permute(far, MIDDLE, n_ep)).astype(bf16)
    dnormed = (
        sums[0]
        + depth_permute(near, MIDDLE, n_ep).astype(jnp.float32)
        + depth_permute(partner, SWAP, n_ep).astype(jnp.float32)
    )

    score_rows = tp_sum(jnp.concatenate(scores)).astype(bf16).astype(jnp.float32)
    score_rows = score_rows.reshape(DEPTH, plane, capacity, 1)
    token_scores = jnp.sum(expert_hot * score_rows, axis=2).reshape(n_ep, length)
    order = jnp.argmax(expert_seq.reshape(1, n_ep) == expert_ids[:, None], axis=1)
    ret_scores = lax.all_to_all(
        token_scores[order].reshape(n_ep, 1, length), "ep", split_axis=0, concat_axis=0, tiled=True
    ).reshape(n_ep, length)
    dweight = jnp.sum(jnp.where(one_hot, ret_scores.T[:, None, :], 0.0), axis=2)

    dpicked = (
        route_scale / totals * (dweight - jnp.sum(dweight * picked, axis=1, keepdims=True) / totals)
    )
    dlogits = jnp.sum(
        jnp.where(one_hot, (dpicked * picked * (1.0 - picked))[:, :, None], 0.0), axis=1
    )
    dnorm_f = dnormed + jnp.dot(dlogits, router_f.T, precision=lax.Precision.HIGHEST)
    gained = gain_f * dnorm_f
    inner_sum = tp_sum(jnp.sum(gained * resid_f, axis=1))[:, None]
    dresid = inv_rms * gained - resid_f * (inv_rms * inv_rms * inv_rms) * inner_sum / D
    grad_in = (grad_out.astype(jnp.float32) + dresid).astype(bf16)
    partial_heads = jnp.einsum("td,hd->th", grad_in, slab, preferred_element_type=jnp.float32)
    grad_attn = tp_reduce(partial_heads.astype(bf16), 1).astype(bf16)
    grad_h = split_heads(grad_attn)
    grad_value = jnp.einsum(
        "hqk,qhd->khd", prob_rounded, grad_h, preferred_element_type=jnp.float32
    )
    grad_prob = jnp.einsum("qhd,khd->hqk", grad_h, value_h, preferred_element_type=jnp.float32)
    centre = jnp.sum(probabilities * grad_prob, axis=2, keepdims=True)
    grad_score = (probabilities * (grad_prob - centre)).astype(bf16)
    grad_query = jnp.einsum(
        "hqk,khd->qhd", grad_score, key_h, preferred_element_type=jnp.float32
    ) * (1.0 / math.sqrt(HDIM))
    grad_key = jnp.einsum(
        "hqk,qhd->khd", grad_score, query_h, preferred_element_type=jnp.float32
    ) * (1.0 / math.sqrt(HDIM))
    return (
        grad_in,
        grad_query.reshape(length, -1).astype(bf16),
        grad_key.reshape(length, -1).astype(bf16),
        grad_value.reshape(length, -1).astype(bf16),
    )


def solution(mesh):
    in_specs = (
        P("ep", "tp"),
        P("ep", "tp"),
        P("ep", "tp"),
        P("ep", "tp"),
        P(None, ("tp", "ep")),
        P("tp"),
        P("tp", None),
        P("ep", None),
        P("ep", "tp", None),
        P("ep", "tp", None),
        P("ep", None, "tp"),
        P("ep", "tp"),
    )
    out_specs = (P("ep", "tp"), P("ep", "tp"), P("ep", "tp"), P("ep", "tp"))
    return jax.shard_map(
        on_device, mesh=mesh, in_specs=in_specs, out_specs=out_specs, check_vma=False
    )
```

```python
import math

import jax
import jax.numpy as jnp
from jax import lax
from jax.sharding import PartitionSpec as P

D = 7168
HDIM = 128
TOP = 8
DEPTH = 4


route_scale = 2.5
norm_eps = 1e-06
masked_score = -1e30


def split_heads(values):
    return values.reshape(values.shape[0], values.shape[1] // HDIM, HDIM)


def softmax_rows(query_h, key_h):
    length = query_h.shape[0]
    scores = jnp.einsum("qhd,khd->hqk", query_h, key_h, preferred_element_type=jnp.float32) * (
        1.0 / math.sqrt(HDIM)
    )
    causal = jnp.arange(length)[None, :] <= jnp.arange(length)[:, None]
    scores = jnp.where(causal[None], scores, masked_score)
    highest = jnp.max(scores, axis=2, keepdims=True)
    weights_exp = jnp.exp(scores - highest)
    return weights_exp / jnp.sum(weights_exp, axis=2, keepdims=True)


def depth_permute(x, pairs, n_ep):
    plane = n_ep // DEPTH
    return lax.ppermute(
        x, "ep", [(a * plane + i, b * plane + i) for a, b in pairs for i in range(plane)]
    )


def plane_permute(x, step, n_ep):
    return lax.ppermute(x, "ep", [(i, i ^ step) for i in range(n_ep)])


SWAP = [(0, 1), (1, 0), (2, 3), (3, 2)]
MIDDLE = [(1, 2), (2, 1)]
OUTWARD = [(1, 0), (2, 3)]
INWARD = [(0, 1), (3, 2)]


class Steps:
    def __init__(self, n_ep):
        self.n_ep = n_ep
        self.held = ()

    def run(self, moves, work=None, inputs=()):
        moving = tuple(x for x, _ in moves)
        moving, inputs, self.held = lax.optimization_barrier((moving, tuple(inputs), self.held))
        arrived = [
            plane_permute(x, way, self.n_ep)
            if isinstance(way, int)
            else depth_permute(x, way, self.n_ep)
            for x, (_, way) in zip(moving, moves)
        ]
        result = () if work is None else work(*inputs)
        arrived, result = lax.optimization_barrier((arrived, result))
        self.held = (arrived, result)
        return arrived if work is None else [*arrived, result]


def to_plane(blocks):
    return [(blocks[r], r) for r in range(1, blocks.shape[0])]


def from_plane(blocks, arrived):
    return jnp.concatenate([blocks[0], *arrived], axis=0)


def tp_swap(x):
    return lax.ppermute(x, "tp", [(0, 1), (1, 0)])


def tp_sum(x):
    if lax.axis_size("tp") != 2:
        return lax.psum(x, "tp")
    return x + tp_swap(x)


def tp_reduce(x, axis):
    n_tp = lax.axis_size("tp")
    if n_tp != 2:
        return lax.psum_scatter(x, "tp", scatter_dimension=axis, tiled=True).astype(jnp.float32)
    t = lax.axis_index("tp")
    width = x.shape[axis] // 2
    mine = lax.dynamic_slice_in_dim(x, t * width, width, axis)
    other = lax.dynamic_slice_in_dim(x, (1 - t) * width, width, axis)
    return mine.astype(jnp.float32) + tp_swap(other).astype(jnp.float32)


def tp_gather(x, axis):
    n_tp = lax.axis_size("tp")
    if n_tp != 2:
        return lax.all_gather(x, "tp", axis=axis, tiled=True)
    t = lax.axis_index("tp")
    other = tp_swap(x)
    first = jnp.where(t == 0, x, other)
    second = jnp.where(t == 0, other, x)
    return jnp.concatenate([first, second], axis=axis)


def one_hot_slots(mask, capacity):
    length = mask.shape[-1]
    before = (jnp.arange(length)[:, None] < jnp.arange(length)[None, :]).astype(jnp.bfloat16)
    slots = jnp.einsum(
        "...i,ij->...j", mask.astype(jnp.bfloat16), before, preferred_element_type=jnp.float32
    )
    wanted = jnp.arange(capacity, dtype=jnp.float32)[:, None]
    return (mask[..., None, :] & (slots[..., None, :] == wanted)).astype(jnp.bfloat16)


def on_device(
    hidden_in,
    query,
    key_in,
    value_in,
    out_weight,
    norm_gain,
    router,
    routes,
    w_gate,
    w_up,
    w_down,
    grad_out,
):
    n_ep = lax.axis_size("ep")
    plane = n_ep // DEPTH
    me = lax.axis_index("ep")
    z, place = me // plane, me % plane
    n_tp, t = lax.axis_size("tp"), lax.axis_index("tp")
    length = hidden_in.shape[0]
    slice_width = hidden_in.shape[1]
    capacity = min(length, (5 * length * TOP + 4 * n_ep - 1) // (4 * n_ep))
    bf16 = jnp.bfloat16

    step = Steps(n_ep)
    steps = jnp.arange(plane, dtype=jnp.int32)
    relay_expert = z * plane + (place ^ steps)
    lanes = -(-2 * n_ep // 128) * 128

    def with_lanes(x, extra):
        extra = jnp.pad(extra.astype(bf16), ((0, 0), (0, lanes - extra.shape[1])))
        return jnp.concatenate([x, extra], axis=1)

    def pack(piece, hot):
        packed = jnp.dot(hot, piece[:, :slice_width], preferred_element_type=jnp.float32)
        return packed.astype(bf16).reshape(plane, capacity, slice_width)

    def slots_of(piece):
        named = piece[:, slice_width : slice_width + TOP].astype(jnp.int32)
        mask = jnp.any(named[None] == relay_expert[:, None, None], axis=-1)
        return one_hot_slots(mask, capacity).reshape(plane * capacity, length)

    gate_local = w_gate[0]
    up_local = w_up[0]
    down_local = w_down[0]

    def gate_up(rows):
        gate_part = jnp.dot(rows, gate_local, preferred_element_type=jnp.float32).astype(bf16)
        up_part = jnp.dot(rows, up_local, preferred_element_type=jnp.float32).astype(bf16)
        return gate_part, up_part

    def backward_part(rows):
        part = jnp.einsum("rd,hd->rh", rows, down_local, preferred_element_type=jnp.float32)
        return part.astype(bf16)

    score_lane = (jnp.arange(lanes) == me)[None, :]

    def expert_rows(gate_part, up_part, back_part):
        pre_sums = tp_reduce(jnp.stack([gate_part, up_part, back_part]), 2)
        gate_pre, up_pre, back = pre_sums[0], pre_sums[1], pre_sums[2]
        gate_sigmoid = jax.nn.sigmoid(gate_pre)
        gate_silu = gate_pre * gate_sigmoid
        hidden_b = lax.optimization_barrier((gate_silu * up_pre).astype(bf16)).astype(jnp.float32)
        score = tp_sum(jnp.sum(hidden_b * back, axis=1))[:, None]
        grad_gate = (back * up_pre * gate_sigmoid * (1.0 + gate_pre * (1.0 - gate_sigmoid))).astype(
            bf16
        )
        grad_up = (back * gate_silu).astype(bf16)
        both = tp_gather(jnp.stack([grad_gate, grad_up]), 2)
        expert_grad = jnp.einsum(
            "rh,dh->rd", both[0], gate_local, preferred_element_type=jnp.float32
        ) + jnp.einsum("rh,dh->rd", both[1], up_local, preferred_element_type=jnp.float32)
        rows = jnp.concatenate(
            [expert_grad.astype(bf16), jnp.where(score_lane, score, 0.0).astype(bf16)], axis=1
        )
        return rows.reshape(plane, capacity, -1)

    def relay_sum(hot, table, arrived):
        arrived = arrived.reshape(plane * capacity, -1)
        high = jnp.take(table, relay_expert, axis=1).T[:, None, :]
        low = jnp.take(table, n_ep + relay_expert, axis=1).T[:, None, :]
        tokens = hot.reshape(plane, capacity, length)
        mix = jnp.concatenate([tokens * high, tokens * low], axis=0).reshape(-1, length)
        row_part = arrived[:, :slice_width]
        total = jnp.einsum(
            "ri,rd->id",
            mix,
            jnp.concatenate([row_part, row_part], axis=0),
            preferred_element_type=jnp.float32,
        )
        lane_part = jnp.einsum(
            "ri,rd->id", hot, arrived[:, slice_width:], preferred_element_type=jnp.float32
        )
        return jnp.concatenate([total, lane_part], axis=1)

    def attend(query, key_in, value_in):
        probabilities = softmax_rows(split_heads(query), split_heads(key_in))
        attended = jnp.einsum(
            "hqk,khd->qhd",
            probabilities.astype(bf16),
            split_heads(value_in),
            preferred_element_type=jnp.float32,
        )
        return probabilities, attended.reshape(length, -1).astype(bf16)

    def slots_pack(piece):
        hot = slots_of(piece)
        return hot, pack(piece, hot)

    grad_own = with_lanes(grad_out, routes)
    hot_own, grad_blocks = slots_pack(grad_own)
    cols_partner, cols_near, *arrived, (probabilities, attended) = step.run(
        [(out_weight, SWAP), (out_weight, MIDDLE)] + to_plane(grad_blocks),
        attend,
        (query, key_in, value_in),
    )
    grad_rows_own = from_plane(grad_blocks, arrived)
    query_h = split_heads(query)
    key_h = split_heads(key_in)
    value_h = split_heads(value_in)
    prob_rounded = probabilities.astype(bf16)
    cols_far, outer, *arrived = step.run(
        [(cols_partner, MIDDLE), (cols_near, OUTWARD)] + [(attended, r) for r in range(1, plane)]
    )
    cols_near = cols_near + outer
    outer, grad_near, heads = step.run(
        [(cols_far, OUTWARD), (grad_own, MIDDLE)],
        lambda *parts: tp_gather(jnp.concatenate(parts, axis=0), 1),
        (attended, *arrived),
    )
    columns = jnp.concatenate([out_weight, cols_partner, cols_near, cols_far + outer], axis=1)
    column_count = out_weight.shape[1]
    sources = jnp.stack([z, z ^ 1, jnp.where(z < 2, 2, 1), jnp.where(z < 2, 3, 0)])
    column_owner = ((place ^ steps)[:, None] + sources[None, :] * plane).reshape(n_ep)
    expert_ids = jnp.arange(n_ep, dtype=jnp.int32)
    order = jnp.argmax(column_owner[None, :] == expert_ids[:, None], axis=1)

    projected = jnp.dot(heads, columns, preferred_element_type=jnp.float32).astype(bf16)
    blocks = projected.reshape(plane, length, DEPTH * column_count)
    grad_partner, *arrived = step.run(
        [(grad_own, SWAP)] + [(blocks[r], r) for r in range(1, plane)]
    )
    proj = jnp.stack([blocks[0], *arrived]).reshape(plane, length, DEPTH, column_count)
    proj = proj.transpose(0, 2, 1, 3).reshape(n_ep, length, column_count)

    def normalise(proj):
        proj = proj[order].transpose(1, 0, 2).reshape(length, slice_width)
        residual = (hidden_in.astype(jnp.float32) + proj.astype(jnp.float32)).astype(bf16)
        resid_f = residual.astype(jnp.float32)
        scaled = resid_f * norm_gain.astype(jnp.float32)
        squares = tp_sum(jnp.sum(resid_f * resid_f, axis=1))
        raw_logits = tp_sum(
            jnp.dot(scaled, router.astype(jnp.float32), precision=lax.Precision.HIGHEST)
        )
        inv_rms = lax.rsqrt(squares[:, None] / D + norm_eps)
        normed = (scaled * inv_rms).astype(bf16)
        one_hot = routes[:, :, None] == expert_ids[None, None, :]
        sigmoids = jax.nn.sigmoid(raw_logits * inv_rms)
        picked = jnp.sum(jnp.where(one_hot, sigmoids[:, None, :], 0.0), axis=2)
        totals = jnp.sum(picked, axis=1, keepdims=True)
        weights = route_scale * picked / totals
        table = jnp.sum(jnp.where(one_hot, weights[:, :, None], 0.0), axis=1)
        high = table.astype(bf16)
        low = (table - high.astype(jnp.float32)).astype(bf16)
        normed = with_lanes(normed, jnp.concatenate([high, low], axis=1))
        return residual, inv_rms, picked, totals, normed, pack(normed, hot_own)

    hot_partner, grad_blocks = slots_pack(grad_partner)
    grad_far, outer, *arrived, made = step.run(
        [(grad_partner, MIDDLE), (grad_near, OUTWARD)] + to_plane(grad_blocks),
        normalise,
        (proj,),
    )
    residual, inv_rms, picked, totals, normed_own, blocks = made
    resid_f = residual.astype(jnp.float32)
    gain_f = norm_gain.astype(jnp.float32)
    router_f = router.astype(jnp.float32)
    one_hot = routes[:, :, None] == expert_ids[None, None, :]
    grad_rows_partner = from_plane(grad_blocks, arrived)
    grad_near = grad_near + outer

    normed_partner, normed_near, *arrived, ((hot_near, grad_blocks), back_own) = step.run(
        [(normed_own, SWAP), (normed_own, MIDDLE)] + to_plane(blocks),
        lambda piece, rows: (slots_pack(piece), backward_part(rows)),
        (grad_near, grad_rows_own),
    )
    rows_own = from_plane(blocks, arrived)
    normed_far, outer, *arrived, (pre_own, blocks) = step.run(
        [(normed_partner, MIDDLE), (normed_near, OUTWARD)] + to_plane(grad_blocks),
        lambda rows, piece, hot: (gate_up(rows), pack(piece, hot)),
        (rows_own, normed_partner, hot_partner),
    )
    grad_rows_near = from_plane(grad_blocks, arrived)
    normed_near = normed_near + outer
    outer, *arrived, (back_partner, near_blocks) = step.run(
        [(grad_far, OUTWARD)] + to_plane(blocks),
        lambda rows, piece, hot: (backward_part(rows), pack(piece, hot)),
        (grad_rows_partner, normed_near, hot_near),
    )
    rows_partner = from_plane(blocks, arrived)
    grad_far = grad_far + outer
    outer, *arrived, (pre_partner, (hot_far, grad_blocks)) = step.run(
        [(normed_far, OUTWARD)] + to_plane(near_blocks),
        lambda rows, piece: (gate_up(rows), slots_pack(piece)),
        (rows_partner, grad_far),
    )
    rows_near = from_plane(near_blocks, arrived)
    normed_far = normed_far + outer
    *arrived, (pre_near, back_near, far_blocks) = step.run(
        to_plane(grad_blocks),
        lambda rows, grads, piece, hot: (gate_up(rows), backward_part(grads), pack(piece, hot)),
        (rows_near, grad_rows_near, normed_far, hot_far),
    )
    grad_rows_far = from_plane(grad_blocks, arrived)
    *arrived, (back_far, own_blocks) = step.run(
        to_plane(far_blocks),
        lambda rows, pre, back: (backward_part(rows), expert_rows(*pre, back)),
        (grad_rows_far, pre_own, back_own),
    )
    rows_far = from_plane(far_blocks, arrived)

    *arrived, (near_blocks, blocks) = step.run(
        to_plane(own_blocks),
        lambda rows, back, pre, near_back: (
            expert_rows(*pre, near_back),
            expert_rows(*gate_up(rows), back),
        ),
        (rows_far, back_far, pre_near, back_near),
    )
    own_arrived = from_plane(own_blocks, arrived)
    *arrived, (own_sum, partner_blocks) = step.run(
        to_plane(blocks),
        lambda got, table, pre, back: (
            relay_sum(hot_own, table, got),
            expert_rows(*pre, back),
        ),
        (own_arrived, normed_own[:, slice_width:], pre_partner, back_partner),
    )
    far_sum = relay_sum(hot_far, normed_far[:, slice_width:], from_plane(blocks, arrived))
    inward, *arrived = step.run([(far_sum.astype(bf16), INWARD)] + to_plane(near_blocks))
    far_sum = (far_sum + inward).astype(bf16)
    near_sum = relay_sum(hot_near, normed_near[:, slice_width:], from_plane(near_blocks, arrived))
    across, inward, *arrived = step.run(
        [(far_sum, MIDDLE), (near_sum.astype(bf16), INWARD)] + to_plane(partner_blocks)
    )
    near_sum = (near_sum + inward).astype(bf16)
    partner_sum = relay_sum(
        hot_partner, normed_partner[:, slice_width:], from_plane(partner_blocks, arrived)
    )
    partner_sum = (partner_sum + across).astype(bf16)
    near_in, partner_in = step.run([(near_sum, MIDDLE), (partner_sum, SWAP)])
    dnormed = own_sum + near_in.astype(jnp.float32) + partner_in.astype(jnp.float32)
    ret_scores = dnormed[:, slice_width : slice_width + n_ep]
    dnormed = dnormed[:, :slice_width]
    dweight = jnp.sum(jnp.where(one_hot, ret_scores[:, None, :], 0.0), axis=2)

    dpicked = (
        route_scale / totals * (dweight - jnp.sum(dweight * picked, axis=1, keepdims=True) / totals)
    )
    dlogits = jnp.sum(
        jnp.where(one_hot, (dpicked * picked * (1.0 - picked))[:, :, None], 0.0), axis=1
    )
    dnorm_f = dnormed + jnp.dot(dlogits, router_f.T, precision=lax.Precision.HIGHEST)
    gained = gain_f * dnorm_f
    inner_sum = tp_sum(jnp.sum(gained * resid_f, axis=1))[:, None]
    dresid = inv_rms * gained - resid_f * (inv_rms * inv_rms * inv_rms) * inner_sum / D
    grad_in = (grad_out.astype(jnp.float32) + dresid).astype(bf16)
    blocks = grad_in.reshape(length, n_ep, column_count).transpose(1, 0, 2)[column_owner]
    blocks = blocks.reshape(plane, DEPTH, length, column_count).transpose(0, 2, 1, 3)
    blocks = blocks.reshape(plane, length, DEPTH * column_count)
    arrived = step.run([(blocks[r], r) for r in range(1, plane)])
    partial_heads = jnp.einsum(
        "td,hd->th",
        jnp.concatenate([blocks[0], *arrived], axis=0),
        columns,
        preferred_element_type=jnp.float32,
    )
    head_sums = tp_reduce(partial_heads.astype(bf16), 1)
    blocks = head_sums.astype(bf16).reshape(plane, length, -1)
    arrived = step.run([(blocks[r], r) for r in range(1, plane)])
    grad_attn = head_sums[:length]
    for part in arrived:
        grad_attn = grad_attn + part.astype(jnp.float32)
    grad_attn = grad_attn.astype(bf16)
    grad_h = split_heads(grad_attn)
    grad_value = jnp.einsum(
        "hqk,qhd->khd", prob_rounded, grad_h, preferred_element_type=jnp.float32
    )
    grad_prob = jnp.einsum("qhd,khd->hqk", grad_h, value_h, preferred_element_type=jnp.float32)
    centre = jnp.sum(probabilities * grad_prob, axis=2, keepdims=True)
    grad_score = (probabilities * (grad_prob - centre)).astype(bf16)
    grad_query = jnp.einsum(
        "hqk,khd->qhd", grad_score, key_h, preferred_element_type=jnp.float32
    ) * (1.0 / math.sqrt(HDIM))
    grad_key = jnp.einsum(
        "hqk,qhd->khd", grad_score, query_h, preferred_element_type=jnp.float32
    ) * (1.0 / math.sqrt(HDIM))
    return (
        grad_in,
        grad_query.reshape(length, -1).astype(bf16),
        grad_key.reshape(length, -1).astype(bf16),
        grad_value.reshape(length, -1).astype(bf16),
    )


def solution(mesh):
    in_specs = (
        P("ep", "tp"),
        P("ep", "tp"),
        P("ep", "tp"),
        P("ep", "tp"),
        P(None, ("tp", "ep")),
        P("tp"),
        P("tp", None),
        P("ep", None),
        P("ep", "tp", None),
        P("ep", "tp", None),
        P("ep", None, "tp"),
        P("ep", "tp"),
    )
    out_specs = (P("ep", "tp"), P("ep", "tp"), P("ep", "tp"), P("ep", "tp"))
    return jax.shard_map(
        on_device, mesh=mesh, in_specs=in_specs, out_specs=out_specs, check_vma=False
    )
```

```python
import math

import jax
import jax.numpy as jnp
from jax import lax
from jax.experimental import pallas as pl
from jax.experimental.pallas import tpu as pltpu
from jax.sharding import PartitionSpec as P

D = 7168
HDIM = 128
TOP = 8
DEPTH = 4


route_scale = 2.5
norm_eps = 1e-06
masked_score = -1e30


def split_heads(values):
    return values.reshape(values.shape[0], values.shape[1] // HDIM, HDIM)


def softmax_rows(query_h, key_h):
    length = query_h.shape[0]
    scores = jnp.einsum("qhd,khd->hqk", query_h, key_h, preferred_element_type=jnp.float32) * (
        1.0 / math.sqrt(HDIM)
    )
    causal = jnp.arange(length)[None, :] <= jnp.arange(length)[:, None]
    scores = jnp.where(causal[None], scores, masked_score)
    highest = jnp.max(scores, axis=2, keepdims=True)
    weights_exp = jnp.exp(scores - highest)
    return weights_exp / jnp.sum(weights_exp, axis=2, keepdims=True)


def depth_permute(x, pairs, n_ep):
    plane = n_ep // DEPTH
    return lax.ppermute(
        x, "ep", [(a * plane + i, b * plane + i) for a, b in pairs for i in range(plane)]
    )


def plane_permute(x, step, n_ep):
    return lax.ppermute(x, "ep", [(i, i ^ step) for i in range(n_ep)])


SWAP = [(0, 1), (1, 0), (2, 3), (3, 2)]
MIDDLE = [(1, 2), (2, 1)]
OUTWARD = [(1, 0), (2, 3)]
INWARD = [(0, 1), (3, 2)]


HINT = pl.CostEstimate(flops=1 << 20, bytes_accessed=1 << 16, transcendentals=0)
PARAMS = pltpu.CompilerParams(vmem_limit_bytes=30 << 20)


def whole(array):
    return pl.BlockSpec(array.shape, lambda i: (0, 0))


def products_kernel(rows_ref, *refs):
    half = len(refs) // 2
    for weight_ref, out_ref in zip(refs[:half], refs[half:]):
        out_ref[...] = jnp.dot(
            rows_ref[...], weight_ref[...], preferred_element_type=jnp.float32
        ).astype(out_ref.dtype)


def products(rows, *weights):
    count, depth = rows.shape
    width = weights[0].shape[1]
    tile = math.gcd(width, 256)
    return pl.pallas_call(
        products_kernel,
        grid=(width // tile,),
        in_specs=[whole(rows)] + [pl.BlockSpec((depth, tile), lambda i: (0, i))] * len(weights),
        out_specs=[pl.BlockSpec((count, tile), lambda i: (0, i))] * len(weights),
        out_shape=[jax.ShapeDtypeStruct((count, width), jnp.bfloat16)] * len(weights),
        compiler_params=PARAMS,
        cost_estimate=HINT,
    )(rows, *weights)


def summed_kernel(*refs):
    half = len(refs) // 2
    total = None
    for rows_ref, weight_ref in zip(refs[:half], refs[half : 2 * half]):
        part = lax.dot_general(
            rows_ref[...],
            weight_ref[...],
            (((1,), (1,)), ((), ())),
            preferred_element_type=jnp.float32,
        )
        total = part if total is None else total + part
    refs[-1][...] = total.astype(refs[-1].dtype)


def summed_products(rows, weights):
    count, depth = rows[0].shape
    height = weights[0].shape[0]
    tile = math.gcd(height, 512 if depth <= 1024 else 256)
    return pl.pallas_call(
        summed_kernel,
        grid=(height // tile,),
        in_specs=[whole(x) for x in rows]
        + [pl.BlockSpec((tile, depth), lambda i: (i, 0))] * len(weights),
        out_specs=pl.BlockSpec((count, tile), lambda i: (0, i)),
        out_shape=jax.ShapeDtypeStruct((count, height), jnp.bfloat16),
        compiler_params=PARAMS,
        cost_estimate=HINT,
    )(*rows, *weights)


class Steps:
    def __init__(self, n_ep):
        self.n_ep = n_ep
        self.held = ()

    def run(self, moves, work=None, inputs=()):
        moving = tuple(x for x, _ in moves)
        moving, inputs, self.held = lax.optimization_barrier((moving, tuple(inputs), self.held))
        arrived = [
            plane_permute(x, way, self.n_ep)
            if isinstance(way, int)
            else depth_permute(x, way, self.n_ep)
            for x, (_, way) in zip(moving, moves)
        ]
        result = () if work is None else work(*inputs)
        arrived, result = lax.optimization_barrier((arrived, result))
        self.held = (arrived, result)
        return arrived if work is None else [*arrived, result]


def to_plane(blocks):
    return [(blocks[r], r) for r in range(1, blocks.shape[0])]


def from_plane(blocks, arrived):
    return jnp.concatenate([blocks[0], *arrived], axis=0)


def tp_swap(x):
    return lax.ppermute(x, "tp", [(0, 1), (1, 0)])


def tp_sum(x):
    if lax.axis_size("tp") != 2:
        return lax.psum(x, "tp")
    return x + tp_swap(x)


def tp_reduce(x, axis):
    n_tp = lax.axis_size("tp")
    if n_tp != 2:
        return lax.psum_scatter(x, "tp", scatter_dimension=axis, tiled=True).astype(jnp.float32)
    t = lax.axis_index("tp")
    width = x.shape[axis] // 2
    mine = lax.dynamic_slice_in_dim(x, t * width, width, axis)
    other = lax.dynamic_slice_in_dim(x, (1 - t) * width, width, axis)
    return mine.astype(jnp.float32) + tp_swap(other).astype(jnp.float32)


def tp_gather(x, axis):
    n_tp = lax.axis_size("tp")
    if n_tp != 2:
        return lax.all_gather(x, "tp", axis=axis, tiled=True)
    t = lax.axis_index("tp")
    other = tp_swap(x)
    first = jnp.where(t == 0, x, other)
    second = jnp.where(t == 0, other, x)
    return jnp.concatenate([first, second], axis=axis)


def one_hot_slots(mask, capacity):
    length = mask.shape[-1]
    before = (jnp.arange(length)[:, None] < jnp.arange(length)[None, :]).astype(jnp.bfloat16)
    slots = jnp.einsum(
        "...i,ij->...j", mask.astype(jnp.bfloat16), before, preferred_element_type=jnp.float32
    )
    wanted = jnp.arange(capacity, dtype=jnp.float32)[:, None]
    return (mask[..., None, :] & (slots[..., None, :] == wanted)).astype(jnp.bfloat16)


def on_device(
    hidden_in,
    query,
    key_in,
    value_in,
    out_weight,
    norm_gain,
    router,
    routes,
    w_gate,
    w_up,
    w_down,
    grad_out,
):
    n_ep = lax.axis_size("ep")
    plane = n_ep // DEPTH
    me = lax.axis_index("ep")
    z, place = me // plane, me % plane
    n_tp, t = lax.axis_size("tp"), lax.axis_index("tp")
    length = hidden_in.shape[0]
    slice_width = hidden_in.shape[1]
    capacity = min(length, (5 * length * TOP + 4 * n_ep - 1) // (4 * n_ep))
    bf16 = jnp.bfloat16

    step = Steps(n_ep)
    steps = jnp.arange(plane, dtype=jnp.int32)
    relay_expert = z * plane + (place ^ steps)
    lanes = -(-(2 * n_ep + TOP) // 128) * 128

    def with_lanes(x, extra):
        extra = jnp.pad(extra.astype(bf16), ((0, 0), (0, lanes - extra.shape[1])))
        return jnp.concatenate([x, extra], axis=1)

    def pack(piece, hot):
        packed = jnp.dot(hot, piece[:, :slice_width], preferred_element_type=jnp.float32)
        return packed.astype(bf16).reshape(plane, capacity, slice_width)

    def slots_of(piece, first=0):
        first += slice_width
        named = piece[:, first : first + TOP].astype(jnp.int32)
        mask = jnp.any(named[None] == relay_expert[:, None, None], axis=-1)
        return one_hot_slots(mask, capacity).reshape(plane * capacity, length)

    gate_local = w_gate[0]
    up_local = w_up[0]
    down_local = w_down[0]

    def gate_up(rows):
        return products(rows, gate_local, up_local)

    def backward_part(rows):
        return summed_products([rows], [down_local])

    score_lane = (jnp.arange(lanes) == me)[None, :]

    def expert_rows(gate_part, up_part, back_part):
        pre_sums = tp_reduce(jnp.stack([gate_part, up_part, back_part]), 2)
        gate_pre, up_pre, back = pre_sums[0], pre_sums[1], pre_sums[2]
        gate_sigmoid = jax.nn.sigmoid(gate_pre)
        gate_silu = gate_pre * gate_sigmoid
        hidden_b = lax.optimization_barrier((gate_silu * up_pre).astype(bf16)).astype(jnp.float32)
        score = tp_sum(jnp.sum(hidden_b * back, axis=1))[:, None]
        grad_gate = (back * up_pre * gate_sigmoid * (1.0 + gate_pre * (1.0 - gate_sigmoid))).astype(
            bf16
        )
        grad_up = (back * gate_silu).astype(bf16)
        both = tp_gather(jnp.stack([grad_gate, grad_up]), 2)
        expert_grad = summed_products([both[0], both[1]], [gate_local, up_local])
        rows = jnp.concatenate(
            [expert_grad, jnp.where(score_lane, score, 0.0).astype(bf16)], axis=1
        )
        return rows.reshape(plane, capacity, -1)

    def relay_sum(hot, table, arrived):
        arrived = arrived.reshape(plane * capacity, -1)
        high = jnp.take(table, relay_expert, axis=1).T[:, None, :]
        low = jnp.take(table, n_ep + relay_expert, axis=1).T[:, None, :]
        tokens = hot.reshape(plane, capacity, length)
        mix = jnp.concatenate([tokens * high, tokens * low], axis=0).reshape(-1, length)
        row_part = arrived[:, :slice_width]
        total = jnp.einsum(
            "ri,rd->id",
            mix,
            jnp.concatenate([row_part, row_part], axis=0),
            preferred_element_type=jnp.float32,
        )
        lane_part = jnp.einsum(
            "ri,rd->id", hot, arrived[:, slice_width:], preferred_element_type=jnp.float32
        )
        return jnp.concatenate([total, lane_part], axis=1)

    def attend(query, key_in, value_in):
        probabilities = softmax_rows(split_heads(query), split_heads(key_in))
        attended = jnp.einsum(
            "hqk,khd->qhd",
            probabilities.astype(bf16),
            split_heads(value_in),
            preferred_element_type=jnp.float32,
        )
        return probabilities, attended.reshape(length, -1).astype(bf16)

    def slots_pack(piece):
        hot = slots_of(piece)
        return hot, pack(piece, hot)

    grad_own = with_lanes(grad_out, routes)
    cols_partner, cols_near, ((probabilities, attended), (hot_own, grad_blocks)) = step.run(
        [(out_weight, SWAP), (out_weight, MIDDLE)],
        lambda *given: (attend(*given[:3]), slots_pack(given[3])),
        (query, key_in, value_in, grad_own),
    )
    query_h = split_heads(query)
    key_h = split_heads(key_in)
    value_h = split_heads(value_in)
    prob_rounded = probabilities.astype(bf16)
    cols_far, outer, *arrived = step.run(
        [(cols_partner, MIDDLE), (cols_near, OUTWARD)] + [(attended, r) for r in range(1, plane)]
    )
    cols_near = cols_near + outer
    outer, *grads, heads = step.run(
        [(cols_far, OUTWARD)] + to_plane(grad_blocks),
        lambda *parts: tp_gather(jnp.concatenate(parts, axis=0), 1),
        (attended, *arrived),
    )
    grad_rows_own = from_plane(grad_blocks, grads)
    columns = jnp.concatenate([out_weight, cols_partner, cols_near, cols_far + outer], axis=1)
    column_count = out_weight.shape[1]
    sources = jnp.stack([z, z ^ 1, jnp.where(z < 2, 2, 1), jnp.where(z < 2, 3, 0)])
    column_owner = ((place ^ steps)[:, None] + sources[None, :] * plane).reshape(n_ep)
    expert_ids = jnp.arange(n_ep, dtype=jnp.int32)
    order = jnp.argmax(column_owner[None, :] == expert_ids[:, None], axis=1)

    projected = jnp.dot(heads, columns, preferred_element_type=jnp.float32).astype(bf16)
    blocks = projected.reshape(plane, length, DEPTH * column_count)
    grad_partner, grad_near, *arrived = step.run(
        [(grad_own, SWAP), (grad_own, MIDDLE)] + [(blocks[r], r) for r in range(1, plane)]
    )
    proj = jnp.stack([blocks[0], *arrived]).reshape(plane, length, DEPTH, column_count)
    proj = proj.transpose(0, 2, 1, 3).reshape(n_ep, length, column_count)

    def normalise(proj):
        proj = proj[order].transpose(1, 0, 2).reshape(length, slice_width)
        residual = (hidden_in.astype(jnp.float32) + proj.astype(jnp.float32)).astype(bf16)
        resid_f = residual.astype(jnp.float32)
        scaled = resid_f * norm_gain.astype(jnp.float32)
        products = jnp.dot(scaled, router.astype(jnp.float32), precision=lax.Precision.HIGHEST)
        squares = jnp.sum(resid_f * resid_f, axis=1, keepdims=True)
        sums = tp_sum(jnp.concatenate([products, squares], axis=1))
        raw_logits, squares = sums[:, :n_ep], sums[:, n_ep:]
        inv_rms = lax.rsqrt(squares / D + norm_eps)
        normed = (scaled * inv_rms).astype(bf16)
        one_hot = routes[:, :, None] == expert_ids[None, None, :]
        sigmoids = jax.nn.sigmoid(raw_logits * inv_rms)
        picked = jnp.sum(jnp.where(one_hot, sigmoids[:, None, :], 0.0), axis=2)
        totals = jnp.sum(picked, axis=1, keepdims=True)
        weights = route_scale * picked / totals
        table = jnp.sum(jnp.where(one_hot, weights[:, :, None], 0.0), axis=1)
        high = table.astype(bf16)
        low = (table - high.astype(jnp.float32)).astype(bf16)
        marks = jnp.concatenate([high, low, routes.astype(bf16)], axis=1)
        return residual, inv_rms, picked, totals, with_lanes(normed, marks)

    hot_partner, grad_blocks = slots_pack(grad_partner)
    outer, *arrived, made = step.run(
        [(grad_near, OUTWARD)] + to_plane(grad_blocks),
        normalise,
        (proj,),
    )
    residual, inv_rms, picked, totals, normed_own = made
    resid_f = residual.astype(jnp.float32)
    gain_f = norm_gain.astype(jnp.float32)
    router_f = router.astype(jnp.float32)
    one_hot = routes[:, :, None] == expert_ids[None, None, :]
    grad_rows_partner = from_plane(grad_blocks, arrived)
    grad_near = grad_near + outer

    hot_near, grad_blocks = slots_pack(grad_near)
    normed_partner, normed_near, *arrived, (back_own, back_partner, own_packed) = step.run(
        [(normed_own, SWAP), (normed_own, MIDDLE)] + to_plane(grad_blocks),
        lambda own, partner, piece, hot: (
            backward_part(own),
            backward_part(partner),
            pack(piece, hot),
        ),
        (grad_rows_own, grad_rows_partner, normed_own, hot_own),
    )
    grad_rows_near = from_plane(grad_blocks, arrived)
    blocks = pack(normed_partner, hot_partner)
    normed_far, outer, *arrived, back_near = step.run(
        [(normed_partner, MIDDLE), (normed_near, OUTWARD)] + to_plane(blocks),
        backward_part,
        (grad_rows_near,),
    )
    rows_partner = from_plane(blocks, arrived)
    normed_near = normed_near + outer
    blocks = pack(normed_near, hot_near)
    outer, grad_far, *arrived, pre_partner = step.run(
        [(normed_far, OUTWARD), (grad_partner, MIDDLE)] + to_plane(blocks),
        gate_up,
        (rows_partner,),
    )
    rows_near = from_plane(blocks, arrived)
    normed_far = normed_far + outer
    hot_far = slots_of(normed_far, 2 * n_ep)
    blocks = pack(normed_far, hot_far)
    outer, *arrived, pre_near = step.run(
        [(grad_far, OUTWARD)] + to_plane(blocks), gate_up, (rows_near,)
    )
    rows_far = from_plane(blocks, arrived)
    blocks = pack(grad_far + outer, hot_far)
    *arrived, pre_far = step.run(to_plane(blocks), gate_up, (rows_far,))
    grad_rows_far = from_plane(blocks, arrived)
    *arrived, blocks = step.run(
        to_plane(own_packed),
        lambda rows, pre: expert_rows(*pre, backward_part(rows)),
        (grad_rows_far, pre_far),
    )
    rows_own = from_plane(own_packed, arrived)

    *arrived, (near_blocks, pre_own) = step.run(
        to_plane(blocks),
        lambda pre, back, rows: (expert_rows(*pre, back), gate_up(rows)),
        (pre_near, back_near, rows_own),
    )
    far_sum = relay_sum(hot_far, normed_far[:, slice_width:], from_plane(blocks, arrived))
    inward, *arrived, partner_blocks = step.run(
        [(far_sum.astype(bf16), INWARD)] + to_plane(near_blocks),
        lambda pre, back: expert_rows(*pre, back),
        (pre_partner, back_partner),
    )
    far_sum = (far_sum + inward).astype(bf16)
    near_sum = relay_sum(hot_near, normed_near[:, slice_width:], from_plane(near_blocks, arrived))
    across, inward, *arrived, own_blocks = step.run(
        [(far_sum, MIDDLE), (near_sum.astype(bf16), INWARD)] + to_plane(partner_blocks),
        lambda pre, back: expert_rows(*pre, back),
        (pre_own, back_own),
    )
    near_sum = (near_sum + inward).astype(bf16)
    partner_sum = relay_sum(
        hot_partner, normed_partner[:, slice_width:], from_plane(partner_blocks, arrived)
    )
    partner_sum = (partner_sum + across).astype(bf16)
    near_in, partner_in, *arrived = step.run(
        [(near_sum, MIDDLE), (partner_sum, SWAP)] + to_plane(own_blocks)
    )
    own_sum = relay_sum(hot_own, normed_own[:, slice_width:], from_plane(own_blocks, arrived))
    dnormed = own_sum + near_in.astype(jnp.float32) + partner_in.astype(jnp.float32)
    ret_scores = dnormed[:, slice_width : slice_width + n_ep]
    dnormed = dnormed[:, :slice_width]
    dweight = jnp.sum(jnp.where(one_hot, ret_scores[:, None, :], 0.0), axis=2)

    dpicked = (
        route_scale / totals * (dweight - jnp.sum(dweight * picked, axis=1, keepdims=True) / totals)
    )
    dlogits = jnp.sum(
        jnp.where(one_hot, (dpicked * picked * (1.0 - picked))[:, :, None], 0.0), axis=1
    )
    dnorm_f = dnormed + jnp.dot(dlogits, router_f.T, precision=lax.Precision.HIGHEST)
    gained = gain_f * dnorm_f
    inner_sum = tp_sum(jnp.sum(gained * resid_f, axis=1))[:, None]
    dresid = inv_rms * gained - resid_f * (inv_rms * inv_rms * inv_rms) * inner_sum / D
    grad_in = (grad_out.astype(jnp.float32) + dresid).astype(bf16)
    blocks = grad_in.reshape(length, n_ep, column_count).transpose(1, 0, 2)[column_owner]
    blocks = blocks.reshape(plane, DEPTH, length, column_count).transpose(0, 2, 1, 3)
    blocks = blocks.reshape(plane, length, DEPTH * column_count)
    arrived = step.run([(blocks[r], r) for r in range(1, plane)])
    partial_heads = jnp.einsum(
        "td,hd->th",
        jnp.concatenate([blocks[0], *arrived], axis=0),
        columns,
        preferred_element_type=jnp.float32,
    )
    head_sums = tp_reduce(partial_heads.astype(bf16), 1)
    blocks = head_sums.astype(bf16).reshape(plane, length, -1)
    arrived = step.run([(blocks[r], r) for r in range(1, plane)])
    grad_attn = head_sums[:length]
    for part in arrived:
        grad_attn = grad_attn + part.astype(jnp.float32)
    grad_attn = grad_attn.astype(bf16)
    grad_h = split_heads(grad_attn)
    grad_value = jnp.einsum(
        "hqk,qhd->khd", prob_rounded, grad_h, preferred_element_type=jnp.float32
    )
    grad_prob = jnp.einsum("qhd,khd->hqk", grad_h, value_h, preferred_element_type=jnp.float32)
    centre = jnp.sum(probabilities * grad_prob, axis=2, keepdims=True)
    grad_score = (probabilities * (grad_prob - centre)).astype(bf16)
    grad_query = jnp.einsum(
        "hqk,khd->qhd", grad_score, key_h, preferred_element_type=jnp.float32
    ) * (1.0 / math.sqrt(HDIM))
    grad_key = jnp.einsum(
        "hqk,qhd->khd", grad_score, query_h, preferred_element_type=jnp.float32
    ) * (1.0 / math.sqrt(HDIM))
    return (
        grad_in,
        grad_query.reshape(length, -1).astype(bf16),
        grad_key.reshape(length, -1).astype(bf16),
        grad_value.reshape(length, -1).astype(bf16),
    )


def solution(mesh):
    in_specs = (
        P("ep", "tp"),
        P("ep", "tp"),
        P("ep", "tp"),
        P("ep", "tp"),
        P(None, ("tp", "ep")),
        P("tp"),
        P("tp", None),
        P("ep", None),
        P("ep", "tp", None),
        P("ep", "tp", None),
        P("ep", None, "tp"),
        P("ep", "tp"),
    )
    out_specs = (P("ep", "tp"), P("ep", "tp"), P("ep", "tp"), P("ep", "tp"))
    return jax.shard_map(
        on_device, mesh=mesh, in_specs=in_specs, out_specs=out_specs, check_vma=False
    )
```

```python
import math

import jax
import jax.numpy as jnp
from jax import lax
from jax.experimental import pallas as pl
from jax.experimental.pallas import tpu as pltpu
from jax.sharding import PartitionSpec as P

D = 7168
HDIM = 128
TOP = 8
DEPTH = 4


route_scale = 2.5
norm_eps = 1e-06
masked_score = -1e30


def split_heads(values):
    return values.reshape(values.shape[0], values.shape[1] // HDIM, HDIM)


def softmax_rows(query_h, key_h):
    length = query_h.shape[0]
    scores = jnp.einsum("qhd,khd->hqk", query_h, key_h, preferred_element_type=jnp.float32) * (
        1.0 / math.sqrt(HDIM)
    )
    causal = jnp.arange(length)[None, :] <= jnp.arange(length)[:, None]
    scores = jnp.where(causal[None], scores, masked_score)
    highest = jnp.max(scores, axis=2, keepdims=True)
    weights_exp = jnp.exp(scores - highest)
    return weights_exp / jnp.sum(weights_exp, axis=2, keepdims=True)


def depth_permute(x, pairs, n_ep):
    plane = n_ep // DEPTH
    return lax.ppermute(
        x, "ep", [(a * plane + i, b * plane + i) for a, b in pairs for i in range(plane)]
    )


def plane_permute(x, step, n_ep):
    return lax.ppermute(x, "ep", [(i, i ^ step) for i in range(n_ep)])


SWAP = [(0, 1), (1, 0), (2, 3), (3, 2)]
MIDDLE = [(1, 2), (2, 1)]
OUTWARD = [(1, 0), (2, 3)]
INWARD = [(0, 1), (3, 2)]


HINT = pl.CostEstimate(flops=1 << 20, bytes_accessed=1 << 16, transcendentals=0)
PARAMS = pltpu.CompilerParams(vmem_limit_bytes=16 << 20)


def whole(array):
    return pl.BlockSpec(array.shape, lambda i: (0, 0))


def products_kernel(rows_ref, *refs):
    half = len(refs) // 2
    for weight_ref, out_ref in zip(refs[:half], refs[half:]):
        out_ref[...] = jnp.dot(
            rows_ref[...], weight_ref[...], preferred_element_type=jnp.float32
        ).astype(out_ref.dtype)


def products(rows, *weights):
    count, depth = rows.shape
    width = weights[0].shape[1]
    tile = math.gcd(width, 256)
    return pl.pallas_call(
        products_kernel,
        grid=(width // tile,),
        in_specs=[whole(rows)] + [pl.BlockSpec((depth, tile), lambda i: (0, i))] * len(weights),
        out_specs=[pl.BlockSpec((count, tile), lambda i: (0, i))] * len(weights),
        out_shape=[jax.ShapeDtypeStruct((count, width), jnp.bfloat16)] * len(weights),
        compiler_params=PARAMS,
        cost_estimate=HINT,
    )(rows, *weights)


def summed_kernel(*refs):
    half = len(refs) // 2
    total = None
    for rows_ref, weight_ref in zip(refs[:half], refs[half : 2 * half]):
        part = lax.dot_general(
            rows_ref[...],
            weight_ref[...],
            (((1,), (1,)), ((), ())),
            preferred_element_type=jnp.float32,
        )
        total = part if total is None else total + part
    refs[-1][...] = total.astype(refs[-1].dtype)


def summed_products(rows, weights):
    count, depth = rows[0].shape
    height = weights[0].shape[0]
    tile = math.gcd(height, 512 if depth <= 1024 else 256)
    return pl.pallas_call(
        summed_kernel,
        grid=(height // tile,),
        in_specs=[whole(x) for x in rows]
        + [pl.BlockSpec((tile, depth), lambda i: (i, 0))] * len(weights),
        out_specs=pl.BlockSpec((count, tile), lambda i: (0, i)),
        out_shape=jax.ShapeDtypeStruct((count, height), jnp.bfloat16),
        compiler_params=PARAMS,
        cost_estimate=HINT,
    )(*rows, *weights)


class Steps:
    def __init__(self, n_ep):
        self.n_ep = n_ep
        self.held = ()

    def run(self, moves, work=None, inputs=()):
        moving = tuple(x for x, _ in moves)
        moving, inputs, self.held = lax.optimization_barrier((moving, tuple(inputs), self.held))
        arrived = [
            plane_permute(x, way, self.n_ep)
            if isinstance(way, int)
            else depth_permute(x, way, self.n_ep)
            for x, (_, way) in zip(moving, moves)
        ]
        result = () if work is None else work(*inputs)
        arrived, result = lax.optimization_barrier((arrived, result))
        self.held = (arrived, result)
        return arrived if work is None else [*arrived, result]


def to_plane(blocks):
    return [(blocks[r], r) for r in range(1, blocks.shape[0])]


def from_plane(blocks, arrived):
    return jnp.concatenate([blocks[0], *arrived], axis=0)


def tp_swap(x):
    return lax.ppermute(x, "tp", [(0, 1), (1, 0)])


def tp_sum(x):
    if lax.axis_size("tp") != 2:
        return lax.psum(x, "tp")
    return x + tp_swap(x)


def tp_reduce(x, axis):
    n_tp = lax.axis_size("tp")
    if n_tp != 2:
        return lax.psum_scatter(x, "tp", scatter_dimension=axis, tiled=True).astype(jnp.float32)
    t = lax.axis_index("tp")
    width = x.shape[axis] // 2
    mine = lax.dynamic_slice_in_dim(x, t * width, width, axis)
    other = lax.dynamic_slice_in_dim(x, (1 - t) * width, width, axis)
    return mine.astype(jnp.float32) + tp_swap(other).astype(jnp.float32)


def tp_gather(x, axis):
    n_tp = lax.axis_size("tp")
    if n_tp != 2:
        return lax.all_gather(x, "tp", axis=axis, tiled=True)
    t = lax.axis_index("tp")
    other = tp_swap(x)
    first = jnp.where(t == 0, x, other)
    second = jnp.where(t == 0, other, x)
    return jnp.concatenate([first, second], axis=axis)


def one_hot_slots(mask, capacity):
    length = mask.shape[-1]
    before = (jnp.arange(length)[:, None] < jnp.arange(length)[None, :]).astype(jnp.bfloat16)
    slots = jnp.einsum(
        "...i,ij->...j", mask.astype(jnp.bfloat16), before, preferred_element_type=jnp.float32
    )
    wanted = jnp.arange(capacity, dtype=jnp.float32)[:, None]
    return (mask[..., None, :] & (slots[..., None, :] == wanted)).astype(jnp.bfloat16)


def on_device(
    hidden_in,
    query,
    key_in,
    value_in,
    out_weight,
    norm_gain,
    router,
    routes,
    w_gate,
    w_up,
    w_down,
    grad_out,
):
    n_ep = lax.axis_size("ep")
    plane = n_ep // DEPTH
    me = lax.axis_index("ep")
    z, place = me // plane, me % plane
    n_tp, t = lax.axis_size("tp"), lax.axis_index("tp")
    length = hidden_in.shape[0]
    slice_width = hidden_in.shape[1]
    capacity = min(length, (5 * length * TOP + 4 * n_ep - 1) // (4 * n_ep))
    bf16 = jnp.bfloat16

    step = Steps(n_ep)
    steps = jnp.arange(plane, dtype=jnp.int32)
    relay_expert = z * plane + (place ^ steps)
    lanes = -(-(2 * n_ep + TOP) // 128) * 128

    def with_lanes(x, extra):
        extra = jnp.pad(extra.astype(bf16), ((0, 0), (0, lanes - extra.shape[1])))
        return jnp.concatenate([x, extra], axis=1)

    def pack(piece, hot):
        packed = jnp.dot(hot, piece[:, :slice_width], preferred_element_type=jnp.float32)
        return packed.astype(bf16).reshape(plane, capacity, slice_width)

    def slots_of(piece, first=0):
        first += slice_width
        named = piece[:, first : first + TOP].astype(jnp.int32)
        mask = jnp.any(named[None] == relay_expert[:, None, None], axis=-1)
        return one_hot_slots(mask, capacity).reshape(plane * capacity, length)

    gate_local = w_gate[0]
    up_local = w_up[0]
    down_local = w_down[0]

    def gate_up(rows):
        return products(rows, gate_local, up_local)

    def backward_part(rows):
        return summed_products([rows], [down_local])

    score_lane = (jnp.arange(lanes) == me)[None, :]

    def expert_rows(gate_part, up_part, back_part):
        pre_sums = tp_reduce(jnp.stack([gate_part, up_part, back_part]), 2)
        gate_pre, up_pre, back = pre_sums[0], pre_sums[1], pre_sums[2]
        gate_sigmoid = jax.nn.sigmoid(gate_pre)
        gate_silu = gate_pre * gate_sigmoid
        hidden_b = lax.optimization_barrier((gate_silu * up_pre).astype(bf16)).astype(jnp.float32)
        score = tp_sum(jnp.sum(hidden_b * back, axis=1))[:, None]
        grad_gate = (back * up_pre * gate_sigmoid * (1.0 + gate_pre * (1.0 - gate_sigmoid))).astype(
            bf16
        )
        grad_up = (back * gate_silu).astype(bf16)
        both = tp_gather(jnp.stack([grad_gate, grad_up]), 2)
        expert_grad = summed_products([both[0], both[1]], [gate_local, up_local])
        rows = jnp.concatenate(
            [expert_grad, jnp.where(score_lane, score, 0.0).astype(bf16)], axis=1
        )
        return rows.reshape(plane, capacity, -1)

    def relay_sum(hot, table, arrived):
        arrived = arrived.reshape(plane * capacity, -1)
        high = jnp.take(table, relay_expert, axis=1).T[:, None, :]
        low = jnp.take(table, n_ep + relay_expert, axis=1).T[:, None, :]
        tokens = hot.reshape(plane, capacity, length)
        mix = jnp.concatenate([tokens * high, tokens * low], axis=0).reshape(-1, length)
        row_part = arrived[:, :slice_width]
        total = jnp.einsum(
            "ri,rd->id",
            mix,
            jnp.concatenate([row_part, row_part], axis=0),
            preferred_element_type=jnp.float32,
        )
        lane_part = jnp.einsum(
            "ri,rd->id", hot, arrived[:, slice_width:], preferred_element_type=jnp.float32
        )
        return jnp.concatenate([total, lane_part], axis=1)

    def attend(query, key_in, value_in):
        probabilities = softmax_rows(split_heads(query), split_heads(key_in))
        attended = jnp.einsum(
            "hqk,khd->qhd",
            probabilities.astype(bf16),
            split_heads(value_in),
            preferred_element_type=jnp.float32,
        )
        return probabilities, attended.reshape(length, -1).astype(bf16)

    def slots_pack(piece):
        hot = slots_of(piece)
        return hot, pack(piece, hot)

    grad_own = with_lanes(grad_out, routes)
    cols_partner, cols_near, ((probabilities, attended), (hot_own, grad_blocks)) = step.run(
        [(out_weight, SWAP), (out_weight, MIDDLE)],
        lambda *given: (attend(*given[:3]), slots_pack(given[3])),
        (query, key_in, value_in, grad_own),
    )
    query_h = split_heads(query)
    key_h = split_heads(key_in)
    value_h = split_heads(value_in)
    prob_rounded = probabilities.astype(bf16)
    cols_far, outer, *arrived = step.run(
        [(cols_partner, MIDDLE), (cols_near, OUTWARD)] + [(attended, r) for r in range(1, plane)]
    )
    cols_near = cols_near + outer
    outer, *grads, heads = step.run(
        [(cols_far, OUTWARD)] + to_plane(grad_blocks),
        lambda *parts: tp_gather(jnp.concatenate(parts, axis=0), 1),
        (attended, *arrived),
    )
    grad_rows_own = from_plane(grad_blocks, grads)
    columns = jnp.concatenate([out_weight, cols_partner, cols_near, cols_far + outer], axis=1)
    column_count = out_weight.shape[1]
    sources = jnp.stack([z, z ^ 1, jnp.where(z < 2, 2, 1), jnp.where(z < 2, 3, 0)])
    column_owner = ((place ^ steps)[:, None] + sources[None, :] * plane).reshape(n_ep)
    expert_ids = jnp.arange(n_ep, dtype=jnp.int32)
    order = jnp.argmax(column_owner[None, :] == expert_ids[:, None], axis=1)

    projected = jnp.dot(heads, columns, preferred_element_type=jnp.float32).astype(bf16)
    blocks = projected.reshape(plane, length, DEPTH * column_count)
    grad_partner, grad_near, *arrived = step.run(
        [(grad_own, SWAP), (grad_own, MIDDLE)] + [(blocks[r], r) for r in range(1, plane)]
    )
    proj = jnp.stack([blocks[0], *arrived]).reshape(plane, length, DEPTH, column_count)
    proj = proj.transpose(0, 2, 1, 3).reshape(n_ep, length, column_count)

    def normalise(proj):
        proj = proj[order].transpose(1, 0, 2).reshape(length, slice_width)
        residual = (hidden_in.astype(jnp.float32) + proj.astype(jnp.float32)).astype(bf16)
        resid_f = residual.astype(jnp.float32)
        scaled = resid_f * norm_gain.astype(jnp.float32)
        products = jnp.dot(scaled, router.astype(jnp.float32), precision=lax.Precision.HIGHEST)
        squares = jnp.sum(resid_f * resid_f, axis=1, keepdims=True)
        sums = tp_sum(jnp.concatenate([products, squares], axis=1))
        raw_logits, squares = sums[:, :n_ep], sums[:, n_ep:]
        inv_rms = lax.rsqrt(squares / D + norm_eps)
        normed = (scaled * inv_rms).astype(bf16)
        one_hot = routes[:, :, None] == expert_ids[None, None, :]
        sigmoids = jax.nn.sigmoid(raw_logits * inv_rms)
        picked = jnp.sum(jnp.where(one_hot, sigmoids[:, None, :], 0.0), axis=2)
        totals = jnp.sum(picked, axis=1, keepdims=True)
        weights = route_scale * picked / totals
        table = jnp.sum(jnp.where(one_hot, weights[:, :, None], 0.0), axis=1)
        high = table.astype(bf16)
        low = (table - high.astype(jnp.float32)).astype(bf16)
        marks = jnp.concatenate([high, low, routes.astype(bf16)], axis=1)
        return residual, inv_rms, picked, totals, with_lanes(normed, marks)

    hot_partner, grad_blocks = slots_pack(grad_partner)
    outer, *arrived, made = step.run(
        [(grad_near, OUTWARD)] + to_plane(grad_blocks),
        normalise,
        (proj,),
    )
    residual, inv_rms, picked, totals, normed_own = made
    resid_f = residual.astype(jnp.float32)
    gain_f = norm_gain.astype(jnp.float32)
    router_f = router.astype(jnp.float32)
    one_hot = routes[:, :, None] == expert_ids[None, None, :]
    grad_rows_partner = from_plane(grad_blocks, arrived)
    grad_near = grad_near + outer

    hot_near, grad_blocks = slots_pack(grad_near)
    normed_partner, normed_near, *arrived, (back_own, back_partner, own_packed) = step.run(
        [(normed_own, SWAP), (normed_own, MIDDLE)] + to_plane(grad_blocks),
        lambda own, partner, piece, hot: (
            backward_part(own),
            backward_part(partner),
            pack(piece, hot),
        ),
        (grad_rows_own, grad_rows_partner, normed_own, hot_own),
    )
    grad_rows_near = from_plane(grad_blocks, arrived)
    blocks = pack(normed_partner, hot_partner)
    normed_far, outer, *arrived, back_near = step.run(
        [(normed_partner, MIDDLE), (normed_near, OUTWARD)] + to_plane(blocks),
        backward_part,
        (grad_rows_near,),
    )
    rows_partner = from_plane(blocks, arrived)
    normed_near = normed_near + outer
    blocks = pack(normed_near, hot_near)
    outer, grad_far, *arrived, pre_partner = step.run(
        [(normed_far, OUTWARD), (grad_partner, MIDDLE)] + to_plane(blocks),
        gate_up,
        (rows_partner,),
    )
    rows_near = from_plane(blocks, arrived)
    normed_far = normed_far + outer
    hot_far = slots_of(normed_far, 2 * n_ep)
    blocks = pack(normed_far, hot_far)
    outer, *arrived, pre_near = step.run(
        [(grad_far, OUTWARD)] + to_plane(blocks), gate_up, (rows_near,)
    )
    rows_far = from_plane(blocks, arrived)
    blocks = pack(grad_far + outer, hot_far)
    *arrived, pre_far = step.run(to_plane(blocks), gate_up, (rows_far,))
    grad_rows_far = from_plane(blocks, arrived)
    *arrived, blocks = step.run(
        to_plane(own_packed),
        lambda rows, pre: expert_rows(*pre, backward_part(rows)),
        (grad_rows_far, pre_far),
    )
    rows_own = from_plane(own_packed, arrived)

    *arrived, (near_blocks, pre_own) = step.run(
        to_plane(blocks),
        lambda pre, back, rows: (expert_rows(*pre, back), gate_up(rows)),
        (pre_near, back_near, rows_own),
    )
    far_sum = relay_sum(hot_far, normed_far[:, slice_width:], from_plane(blocks, arrived))
    inward, *arrived, partner_blocks = step.run(
        [(far_sum.astype(bf16), INWARD)] + to_plane(near_blocks),
        lambda pre, back: expert_rows(*pre, back),
        (pre_partner, back_partner),
    )
    far_sum = (far_sum + inward).astype(bf16)
    near_sum = relay_sum(hot_near, normed_near[:, slice_width:], from_plane(near_blocks, arrived))
    across, inward, *arrived, own_blocks = step.run(
        [(far_sum, MIDDLE), (near_sum.astype(bf16), INWARD)] + to_plane(partner_blocks),
        lambda pre, back: expert_rows(*pre, back),
        (pre_own, back_own),
    )
    near_sum = (near_sum + inward).astype(bf16)
    partner_sum = relay_sum(
        hot_partner, normed_partner[:, slice_width:], from_plane(partner_blocks, arrived)
    )
    partner_sum = (partner_sum + across).astype(bf16)
    near_in, partner_in, *arrived = step.run(
        [(near_sum, MIDDLE), (partner_sum, SWAP)] + to_plane(own_blocks)
    )
    own_sum = relay_sum(hot_own, normed_own[:, slice_width:], from_plane(own_blocks, arrived))
    dnormed = own_sum + near_in.astype(jnp.float32) + partner_in.astype(jnp.float32)
    ret_scores = dnormed[:, slice_width : slice_width + n_ep]
    dnormed = dnormed[:, :slice_width]
    dweight = jnp.sum(jnp.where(one_hot, ret_scores[:, None, :], 0.0), axis=2)

    dpicked = (
        route_scale / totals * (dweight - jnp.sum(dweight * picked, axis=1, keepdims=True) / totals)
    )
    dlogits = jnp.sum(
        jnp.where(one_hot, (dpicked * picked * (1.0 - picked))[:, :, None], 0.0), axis=1
    )
    dnorm_f = dnormed + jnp.dot(dlogits, router_f.T, precision=lax.Precision.HIGHEST)
    gained = gain_f * dnorm_f
    inner_sum = tp_sum(jnp.sum(gained * resid_f, axis=1))[:, None]
    dresid = inv_rms * gained - resid_f * (inv_rms * inv_rms * inv_rms) * inner_sum / D
    grad_in = (grad_out.astype(jnp.float32) + dresid).astype(bf16)
    blocks = grad_in.reshape(length, n_ep, column_count).transpose(1, 0, 2)[column_owner]
    blocks = blocks.reshape(plane, DEPTH, length, column_count).transpose(0, 2, 1, 3)
    blocks = blocks.reshape(plane, length, DEPTH * column_count)
    arrived = step.run([(blocks[r], r) for r in range(1, plane)])
    partial_heads = jnp.einsum(
        "td,hd->th",
        jnp.concatenate([blocks[0], *arrived], axis=0),
        columns,
        preferred_element_type=jnp.float32,
    )
    head_sums = tp_reduce(partial_heads.astype(bf16), 1)
    blocks = head_sums.astype(bf16).reshape(plane, length, -1)
    arrived = step.run([(blocks[r], r) for r in range(1, plane)])
    grad_attn = head_sums[:length]
    for part in arrived:
        grad_attn = grad_attn + part.astype(jnp.float32)
    grad_attn = grad_attn.astype(bf16)
    grad_h = split_heads(grad_attn)
    grad_value = jnp.einsum(
        "hqk,qhd->khd", prob_rounded, grad_h, preferred_element_type=jnp.float32
    )
    grad_prob = jnp.einsum("qhd,khd->hqk", grad_h, value_h, preferred_element_type=jnp.float32)
    centre = jnp.sum(probabilities * grad_prob, axis=2, keepdims=True)
    grad_score = (probabilities * (grad_prob - centre)).astype(bf16)
    grad_query = jnp.einsum(
        "hqk,khd->qhd", grad_score, key_h, preferred_element_type=jnp.float32
    ) * (1.0 / math.sqrt(HDIM))
    grad_key = jnp.einsum(
        "hqk,qhd->khd", grad_score, query_h, preferred_element_type=jnp.float32
    ) * (1.0 / math.sqrt(HDIM))
    return (
        grad_in,
        grad_query.reshape(length, -1).astype(bf16),
        grad_key.reshape(length, -1).astype(bf16),
        grad_value.reshape(length, -1).astype(bf16),
    )


def solution(mesh):
    in_specs = (
        P("ep", "tp"),
        P("ep", "tp"),
        P("ep", "tp"),
        P("ep", "tp"),
        P(None, ("tp", "ep")),
        P("tp"),
        P("tp", None),
        P("ep", None),
        P("ep", "tp", None),
        P("ep", "tp", None),
        P("ep", None, "tp"),
        P("ep", "tp"),
    )
    out_specs = (P("ep", "tp"), P("ep", "tp"), P("ep", "tp"), P("ep", "tp"))
    return jax.shard_map(
        on_device, mesh=mesh, in_specs=in_specs, out_specs=out_specs, check_vma=False
    )
```

```python
import math

import jax
import jax.numpy as jnp
from jax import lax
from jax.experimental import pallas as pl
from jax.experimental.pallas import tpu as pltpu
from jax.sharding import PartitionSpec as P

D = 7168
HDIM = 128
TOP = 8
DEPTH = 4


route_scale = 2.5
norm_eps = 1e-06
masked_score = -1e30


def split_heads(values):
    return values.reshape(values.shape[0], values.shape[1] // HDIM, HDIM)


def softmax_rows(query_h, key_h):
    length = query_h.shape[0]
    scores = jnp.einsum("qhd,khd->hqk", query_h, key_h, preferred_element_type=jnp.float32) * (
        1.0 / math.sqrt(HDIM)
    )
    causal = jnp.arange(length)[None, :] <= jnp.arange(length)[:, None]
    scores = jnp.where(causal[None], scores, masked_score)
    highest = jnp.max(scores, axis=2, keepdims=True)
    weights_exp = jnp.exp(scores - highest)
    return weights_exp / jnp.sum(weights_exp, axis=2, keepdims=True)


def depth_permute(x, pairs, n_ep):
    plane = n_ep // DEPTH
    return lax.ppermute(
        x, "ep", [(a * plane + i, b * plane + i) for a, b in pairs for i in range(plane)]
    )


def plane_permute(x, step, n_ep):
    return lax.ppermute(x, "ep", [(i, i ^ step) for i in range(n_ep)])


SWAP = [(0, 1), (1, 0), (2, 3), (3, 2)]
MIDDLE = [(1, 2), (2, 1)]
OUTWARD = [(1, 0), (2, 3)]
INWARD = [(0, 1), (3, 2)]


HINT = pl.CostEstimate(flops=1 << 20, bytes_accessed=1 << 16, transcendentals=0)
PARAMS = pltpu.CompilerParams(vmem_limit_bytes=16 << 20)


def whole(array):
    return pl.BlockSpec(array.shape, lambda i: (0, 0))


def products_kernel(rows_ref, *refs):
    half = len(refs) // 2
    for weight_ref, out_ref in zip(refs[:half], refs[half:]):
        out_ref[...] = jnp.dot(
            rows_ref[...], weight_ref[...], preferred_element_type=jnp.float32
        ).astype(out_ref.dtype)


def products(rows, *weights):
    count, depth = rows.shape
    width = weights[0].shape[1]
    tile = math.gcd(width, 256)
    return pl.pallas_call(
        products_kernel,
        grid=(width // tile,),
        in_specs=[whole(rows)] + [pl.BlockSpec((depth, tile), lambda i: (0, i))] * len(weights),
        out_specs=[pl.BlockSpec((count, tile), lambda i: (0, i))] * len(weights),
        out_shape=[jax.ShapeDtypeStruct((count, width), jnp.bfloat16)] * len(weights),
        compiler_params=PARAMS,
        cost_estimate=HINT,
    )(rows, *weights)


def summed_kernel(*refs):
    half = len(refs) // 2
    total = None
    for rows_ref, weight_ref in zip(refs[:half], refs[half : 2 * half]):
        part = lax.dot_general(
            rows_ref[...],
            weight_ref[...],
            (((1,), (1,)), ((), ())),
            preferred_element_type=jnp.float32,
        )
        total = part if total is None else total + part
    refs[-1][...] = total.astype(refs[-1].dtype)


def summed_products(rows, weights):
    count, depth = rows[0].shape
    height = weights[0].shape[0]
    tile = math.gcd(height, 512 if depth <= 1024 else 256)
    return pl.pallas_call(
        summed_kernel,
        grid=(height // tile,),
        in_specs=[whole(x) for x in rows]
        + [pl.BlockSpec((tile, depth), lambda i: (i, 0))] * len(weights),
        out_specs=pl.BlockSpec((count, tile), lambda i: (0, i)),
        out_shape=jax.ShapeDtypeStruct((count, height), jnp.bfloat16),
        compiler_params=PARAMS,
        cost_estimate=HINT,
    )(*rows, *weights)


class Steps:
    def __init__(self, n_ep):
        self.n_ep = n_ep
        self.held = ()

    def run(self, moves, work=None, inputs=()):
        moving = tuple(x for x, _ in moves)
        moving, inputs, self.held = lax.optimization_barrier((moving, tuple(inputs), self.held))
        arrived = [
            plane_permute(x, way, self.n_ep)
            if isinstance(way, int)
            else depth_permute(x, way, self.n_ep)
            for x, (_, way) in zip(moving, moves)
        ]
        result = () if work is None else work(*inputs)
        arrived, result = lax.optimization_barrier((arrived, result))
        self.held = (arrived, result)
        return arrived if work is None else [*arrived, result]


def to_plane(blocks):
    return [(blocks[r], r) for r in range(1, blocks.shape[0])]


def from_plane(blocks, arrived):
    return jnp.concatenate([blocks[0], *arrived], axis=0)


def tp_swap(x):
    return lax.ppermute(x, "tp", [(0, 1), (1, 0)])


def tp_sum(x):
    if lax.axis_size("tp") != 2:
        return lax.psum(x, "tp")
    return x + tp_swap(x)


def tp_reduce(x, axis):
    n_tp = lax.axis_size("tp")
    if n_tp != 2:
        return lax.psum_scatter(x, "tp", scatter_dimension=axis, tiled=True).astype(jnp.float32)
    t = lax.axis_index("tp")
    width = x.shape[axis] // 2
    mine = lax.dynamic_slice_in_dim(x, t * width, width, axis)
    other = lax.dynamic_slice_in_dim(x, (1 - t) * width, width, axis)
    return mine.astype(jnp.float32) + tp_swap(other).astype(jnp.float32)


def tp_gather(x, axis):
    n_tp = lax.axis_size("tp")
    if n_tp != 2:
        return lax.all_gather(x, "tp", axis=axis, tiled=True)
    t = lax.axis_index("tp")
    other = tp_swap(x)
    first = jnp.where(t == 0, x, other)
    second = jnp.where(t == 0, other, x)
    return jnp.concatenate([first, second], axis=axis)


def one_hot_slots(mask, capacity):
    length = mask.shape[-1]
    before = (jnp.arange(length)[:, None] < jnp.arange(length)[None, :]).astype(jnp.bfloat16)
    slots = jnp.einsum(
        "...i,ij->...j", mask.astype(jnp.bfloat16), before, preferred_element_type=jnp.float32
    )
    wanted = jnp.arange(capacity, dtype=jnp.float32)[:, None]
    return (mask[..., None, :] & (slots[..., None, :] == wanted)).astype(jnp.bfloat16)


def on_device(
    hidden_in,
    query,
    key_in,
    value_in,
    out_weight,
    norm_gain,
    router,
    routes,
    w_gate,
    w_up,
    w_down,
    grad_out,
):
    n_ep = lax.axis_size("ep")
    plane = n_ep // DEPTH
    me = lax.axis_index("ep")
    z, place = me // plane, me % plane
    n_tp, t = lax.axis_size("tp"), lax.axis_index("tp")
    length = hidden_in.shape[0]
    slice_width = hidden_in.shape[1]
    capacity = min(length, (5 * length * TOP + 4 * n_ep - 1) // (4 * n_ep))
    bf16 = jnp.bfloat16

    step = Steps(n_ep)
    steps = jnp.arange(plane, dtype=jnp.int32)
    relay_expert = z * plane + (place ^ steps)
    lanes = -(-(n_ep + TOP) // 128) * 128

    def with_lanes(x, extra):
        extra = jnp.pad(extra.astype(bf16), ((0, 0), (0, lanes - extra.shape[1])))
        return jnp.concatenate([x, extra], axis=1)

    def pack(piece, hot):
        packed = jnp.dot(hot, piece[:, :slice_width], preferred_element_type=jnp.float32)
        return packed.astype(bf16).reshape(plane, capacity, slice_width)

    def slots_of(piece, first=0):
        first += slice_width
        named = piece[:, first : first + TOP].astype(jnp.int32)
        mask = jnp.any(named[None] == relay_expert[:, None, None], axis=-1)
        return one_hot_slots(mask, capacity).reshape(plane * capacity, length)

    gate_local = w_gate[0]
    up_local = w_up[0]
    down_local = w_down[0]

    def gate_up(rows):
        return products(rows, gate_local, up_local)

    def backward_part(rows):
        return summed_products([rows], [down_local])

    score_lane = (jnp.arange(lanes) == me)[None, :]

    def expert_rows(gate_part, up_part, back_part):
        pre_sums = tp_reduce(jnp.stack([gate_part, up_part, back_part]), 2)
        gate_pre, up_pre, back = pre_sums[0], pre_sums[1], pre_sums[2]
        gate_sigmoid = jax.nn.sigmoid(gate_pre)
        gate_silu = gate_pre * gate_sigmoid
        hidden_b = lax.optimization_barrier((gate_silu * up_pre).astype(bf16)).astype(jnp.float32)
        score = tp_sum(jnp.sum(hidden_b * back, axis=1))[:, None]
        grad_gate = (back * up_pre * gate_sigmoid * (1.0 + gate_pre * (1.0 - gate_sigmoid))).astype(
            bf16
        )
        grad_up = (back * gate_silu).astype(bf16)
        both = tp_gather(jnp.stack([grad_gate, grad_up]), 2)
        expert_grad = summed_products([both[0], both[1]], [gate_local, up_local])
        rows = jnp.concatenate(
            [expert_grad, jnp.where(score_lane, score, 0.0).astype(bf16)], axis=1
        )
        return rows.reshape(plane, capacity, -1)

    def relay_sum(hot, table, arrived):
        arrived = arrived.reshape(plane * capacity, -1)
        picked_weights = jnp.take(table, relay_expert, axis=1).T[:, None, :]
        tokens = hot.reshape(plane, capacity, length)
        mix = (tokens * picked_weights).reshape(-1, length)
        total = jnp.einsum(
            "ri,rd->id", mix, arrived[:, :slice_width], preferred_element_type=jnp.float32
        )
        lane_part = jnp.einsum(
            "ri,rd->id", hot, arrived[:, slice_width:], preferred_element_type=jnp.float32
        )
        return jnp.concatenate([total, lane_part], axis=1)

    def attend(query, key_in, value_in):
        probabilities = softmax_rows(split_heads(query), split_heads(key_in))
        attended = jnp.einsum(
            "hqk,khd->qhd",
            probabilities.astype(bf16),
            split_heads(value_in),
            preferred_element_type=jnp.float32,
        )
        return probabilities, attended.reshape(length, -1).astype(bf16)

    def slots_pack(piece):
        hot = slots_of(piece)
        return hot, pack(piece, hot)

    grad_own = with_lanes(grad_out, routes)
    cols_partner, cols_near, ((probabilities, attended), (hot_own, grad_blocks)) = step.run(
        [(out_weight, SWAP), (out_weight, MIDDLE)],
        lambda *given: (attend(*given[:3]), slots_pack(given[3])),
        (query, key_in, value_in, grad_own),
    )
    query_h = split_heads(query)
    key_h = split_heads(key_in)
    value_h = split_heads(value_in)
    prob_rounded = probabilities.astype(bf16)
    cols_far, outer, *arrived = step.run(
        [(cols_partner, MIDDLE), (cols_near, OUTWARD)] + [(attended, r) for r in range(1, plane)]
    )
    cols_near = cols_near + outer
    outer, *grads, heads = step.run(
        [(cols_far, OUTWARD)] + to_plane(grad_blocks),
        lambda *parts: tp_gather(jnp.concatenate(parts, axis=0), 1),
        (attended, *arrived),
    )
    grad_rows_own = from_plane(grad_blocks, grads)
    columns = jnp.concatenate([out_weight, cols_partner, cols_near, cols_far + outer], axis=1)
    column_count = out_weight.shape[1]
    sources = jnp.stack([z, z ^ 1, jnp.where(z < 2, 2, 1), jnp.where(z < 2, 3, 0)])
    column_owner = ((place ^ steps)[:, None] + sources[None, :] * plane).reshape(n_ep)
    expert_ids = jnp.arange(n_ep, dtype=jnp.int32)
    order = jnp.argmax(column_owner[None, :] == expert_ids[:, None], axis=1)

    projected = jnp.dot(heads, columns, preferred_element_type=jnp.float32).astype(bf16)
    blocks = projected.reshape(plane, length, DEPTH * column_count)
    grad_partner, grad_near, *arrived = step.run(
        [(grad_own, SWAP), (grad_own, MIDDLE)] + [(blocks[r], r) for r in range(1, plane)]
    )
    proj = jnp.stack([blocks[0], *arrived]).reshape(plane, length, DEPTH, column_count)
    proj = proj.transpose(0, 2, 1, 3).reshape(n_ep, length, column_count)

    def normalise(proj):
        proj = proj[order].transpose(1, 0, 2).reshape(length, slice_width)
        residual = (hidden_in.astype(jnp.float32) + proj.astype(jnp.float32)).astype(bf16)
        resid_f = residual.astype(jnp.float32)
        scaled = resid_f * norm_gain.astype(jnp.float32)
        products = jnp.dot(scaled, router.astype(jnp.float32), precision=lax.Precision.HIGHEST)
        squares = jnp.sum(resid_f * resid_f, axis=1, keepdims=True)
        sums = tp_sum(jnp.concatenate([products, squares], axis=1))
        raw_logits, squares = sums[:, :n_ep], sums[:, n_ep:]
        inv_rms = lax.rsqrt(squares / D + norm_eps)
        normed = (scaled * inv_rms).astype(bf16)
        one_hot = routes[:, :, None] == expert_ids[None, None, :]
        sigmoids = jax.nn.sigmoid(raw_logits * inv_rms)
        picked = jnp.sum(jnp.where(one_hot, sigmoids[:, None, :], 0.0), axis=2)
        totals = jnp.sum(picked, axis=1, keepdims=True)
        weights = route_scale * picked / totals
        table = jnp.sum(jnp.where(one_hot, weights[:, :, None], 0.0), axis=1)
        marks = jnp.concatenate([table.astype(bf16), routes.astype(bf16)], axis=1)
        return residual, inv_rms, picked, totals, with_lanes(normed, marks)

    hot_partner, grad_blocks = slots_pack(grad_partner)
    outer, *arrived, made = step.run(
        [(grad_near, OUTWARD)] + to_plane(grad_blocks),
        normalise,
        (proj,),
    )
    residual, inv_rms, picked, totals, normed_own = made
    resid_f = residual.astype(jnp.float32)
    gain_f = norm_gain.astype(jnp.float32)
    router_f = router.astype(jnp.float32)
    one_hot = routes[:, :, None] == expert_ids[None, None, :]
    grad_rows_partner = from_plane(grad_blocks, arrived)
    grad_near = grad_near + outer

    hot_near, grad_blocks = slots_pack(grad_near)
    normed_partner, normed_near, *arrived, (back_own, back_partner, own_packed) = step.run(
        [(normed_own, SWAP), (normed_own, MIDDLE)] + to_plane(grad_blocks),
        lambda own, partner, piece, hot: (
            backward_part(own),
            backward_part(partner),
            pack(piece, hot),
        ),
        (grad_rows_own, grad_rows_partner, normed_own, hot_own),
    )
    grad_rows_near = from_plane(grad_blocks, arrived)
    blocks = pack(normed_partner, hot_partner)
    normed_far, outer, *arrived, back_near = step.run(
        [(normed_partner, MIDDLE), (normed_near, OUTWARD)] + to_plane(blocks),
        backward_part,
        (grad_rows_near,),
    )
    rows_partner = from_plane(blocks, arrived)
    normed_near = normed_near + outer
    blocks = pack(normed_near, hot_near)
    outer, grad_far, *arrived, pre_partner = step.run(
        [(normed_far, OUTWARD), (grad_partner, MIDDLE)] + to_plane(blocks),
        gate_up,
        (rows_partner,),
    )
    rows_near = from_plane(blocks, arrived)
    normed_far = normed_far + outer
    hot_far = slots_of(normed_far, n_ep)
    blocks = pack(normed_far, hot_far)
    outer, *arrived, pre_near = step.run(
        [(grad_far, OUTWARD)] + to_plane(blocks), gate_up, (rows_near,)
    )
    rows_far = from_plane(blocks, arrived)
    blocks = pack(grad_far + outer, hot_far)
    *arrived, pre_far = step.run(to_plane(blocks), gate_up, (rows_far,))
    grad_rows_far = from_plane(blocks, arrived)
    *arrived, blocks = step.run(
        to_plane(own_packed),
        lambda rows, pre: expert_rows(*pre, backward_part(rows)),
        (grad_rows_far, pre_far),
    )
    rows_own = from_plane(own_packed, arrived)

    *arrived, (near_blocks, pre_own) = step.run(
        to_plane(blocks),
        lambda pre, back, rows: (expert_rows(*pre, back), gate_up(rows)),
        (pre_near, back_near, rows_own),
    )
    far_sum = relay_sum(hot_far, normed_far[:, slice_width:], from_plane(blocks, arrived))
    inward, *arrived, partner_blocks = step.run(
        [(far_sum.astype(bf16), INWARD)] + to_plane(near_blocks),
        lambda pre, back: expert_rows(*pre, back),
        (pre_partner, back_partner),
    )
    far_sum = (far_sum + inward).astype(bf16)
    near_sum = relay_sum(hot_near, normed_near[:, slice_width:], from_plane(near_blocks, arrived))
    across, inward, *arrived, own_blocks = step.run(
        [(far_sum, MIDDLE), (near_sum.astype(bf16), INWARD)] + to_plane(partner_blocks),
        lambda pre, back: expert_rows(*pre, back),
        (pre_own, back_own),
    )
    near_sum = (near_sum + inward).astype(bf16)
    partner_sum = relay_sum(
        hot_partner, normed_partner[:, slice_width:], from_plane(partner_blocks, arrived)
    )
    partner_sum = (partner_sum + across).astype(bf16)
    near_in, partner_in, *arrived = step.run(
        [(near_sum, MIDDLE), (partner_sum, SWAP)] + to_plane(own_blocks)
    )
    own_sum = relay_sum(hot_own, normed_own[:, slice_width:], from_plane(own_blocks, arrived))
    dnormed = own_sum + near_in.astype(jnp.float32) + partner_in.astype(jnp.float32)
    ret_scores = dnormed[:, slice_width : slice_width + n_ep]
    dnormed = dnormed[:, :slice_width]
    dweight = jnp.sum(jnp.where(one_hot, ret_scores[:, None, :], 0.0), axis=2)

    dpicked = (
        route_scale / totals * (dweight - jnp.sum(dweight * picked, axis=1, keepdims=True) / totals)
    )
    dlogits = jnp.sum(
        jnp.where(one_hot, (dpicked * picked * (1.0 - picked))[:, :, None], 0.0), axis=1
    )
    dnorm_f = dnormed + jnp.dot(dlogits, router_f.T, precision=lax.Precision.HIGHEST)
    gained = gain_f * dnorm_f
    inner_sum = tp_sum(jnp.sum(gained * resid_f, axis=1))[:, None]
    dresid = inv_rms * gained - resid_f * (inv_rms * inv_rms * inv_rms) * inner_sum / D
    grad_in = (grad_out.astype(jnp.float32) + dresid).astype(bf16)
    blocks = grad_in.reshape(length, n_ep, column_count).transpose(1, 0, 2)[column_owner]
    blocks = blocks.reshape(plane, DEPTH, length, column_count).transpose(0, 2, 1, 3)
    blocks = blocks.reshape(plane, length, DEPTH * column_count)
    arrived = step.run([(blocks[r], r) for r in range(1, plane)])
    partial_heads = jnp.einsum(
        "td,hd->th",
        jnp.concatenate([blocks[0], *arrived], axis=0),
        columns,
        preferred_element_type=jnp.float32,
    )
    head_sums = tp_reduce(partial_heads.astype(bf16), 1)
    blocks = head_sums.astype(bf16).reshape(plane, length, -1)
    arrived = step.run([(blocks[r], r) for r in range(1, plane)])
    grad_attn = head_sums[:length]
    for part in arrived:
        grad_attn = grad_attn + part.astype(jnp.float32)
    grad_attn = grad_attn.astype(bf16)
    grad_h = split_heads(grad_attn)
    grad_value = jnp.einsum(
        "hqk,qhd->khd", prob_rounded, grad_h, preferred_element_type=jnp.float32
    )
    grad_prob = jnp.einsum("qhd,khd->hqk", grad_h, value_h, preferred_element_type=jnp.float32)
    centre = jnp.sum(probabilities * grad_prob, axis=2, keepdims=True)
    grad_score = (probabilities * (grad_prob - centre)).astype(bf16)
    grad_query = jnp.einsum(
        "hqk,khd->qhd", grad_score, key_h, preferred_element_type=jnp.float32
    ) * (1.0 / math.sqrt(HDIM))
    grad_key = jnp.einsum(
        "hqk,qhd->khd", grad_score, query_h, preferred_element_type=jnp.float32
    ) * (1.0 / math.sqrt(HDIM))
    return (
        grad_in,
        grad_query.reshape(length, -1).astype(bf16),
        grad_key.reshape(length, -1).astype(bf16),
        grad_value.reshape(length, -1).astype(bf16),
    )


def solution(mesh):
    in_specs = (
        P("ep", "tp"),
        P("ep", "tp"),
        P("ep", "tp"),
        P("ep", "tp"),
        P(None, ("tp", "ep")),
        P("tp"),
        P("tp", None),
        P("ep", None),
        P("ep", "tp", None),
        P("ep", "tp", None),
        P("ep", None, "tp"),
        P("ep", "tp"),
    )
    out_specs = (P("ep", "tp"), P("ep", "tp"), P("ep", "tp"), P("ep", "tp"))
    return jax.shard_map(
        on_device, mesh=mesh, in_specs=in_specs, out_specs=out_specs, check_vma=False
    )
```

```python
import math

import jax
import jax.numpy as jnp
from jax import lax
from jax.experimental import pallas as pl
from jax.experimental.pallas import tpu as pltpu
from jax.sharding import PartitionSpec as P

D = 7168
HDIM = 128
TOP = 8
DEPTH = 4


route_scale = 2.5
norm_eps = 1e-06
masked_score = -1e30


def split_heads(values):
    return values.reshape(values.shape[0], values.shape[1] // HDIM, HDIM)


def softmax_rows(query_h, key_h):
    length = query_h.shape[0]
    scores = jnp.einsum("qhd,khd->hqk", query_h, key_h, preferred_element_type=jnp.float32) * (
        1.0 / math.sqrt(HDIM)
    )
    causal = jnp.arange(length)[None, :] <= jnp.arange(length)[:, None]
    scores = jnp.where(causal[None], scores, masked_score)
    highest = jnp.max(scores, axis=2, keepdims=True)
    weights_exp = jnp.exp(scores - highest)
    return weights_exp / jnp.sum(weights_exp, axis=2, keepdims=True)


def depth_permute(x, pairs, n_ep):
    plane = n_ep // DEPTH
    return lax.ppermute(
        x, "ep", [(a * plane + i, b * plane + i) for a, b in pairs for i in range(plane)]
    )


def plane_permute(x, step, n_ep):
    return lax.ppermute(x, "ep", [(i, i ^ step) for i in range(n_ep)])


SWAP = [(0, 1), (1, 0), (2, 3), (3, 2)]
MIDDLE = [(1, 2), (2, 1)]
OUTWARD = [(1, 0), (2, 3)]
INWARD = [(0, 1), (3, 2)]


HINT = pl.CostEstimate(flops=1 << 20, bytes_accessed=1 << 16, transcendentals=0)
PARAMS = pltpu.CompilerParams(vmem_limit_bytes=16 << 20)


def whole(array):
    return pl.BlockSpec(array.shape, lambda i: (0, 0))


def products_kernel(rows_ref, *refs):
    half = len(refs) // 2
    for weight_ref, out_ref in zip(refs[:half], refs[half:]):
        out_ref[...] = jnp.dot(
            rows_ref[...], weight_ref[...], preferred_element_type=jnp.float32
        ).astype(out_ref.dtype)


def products(rows, *weights):
    count, depth = rows.shape
    width = weights[0].shape[1]
    tile = math.gcd(width, 256)
    return pl.pallas_call(
        products_kernel,
        grid=(width // tile,),
        in_specs=[whole(rows)] + [pl.BlockSpec((depth, tile), lambda i: (0, i))] * len(weights),
        out_specs=[pl.BlockSpec((count, tile), lambda i: (0, i))] * len(weights),
        out_shape=[jax.ShapeDtypeStruct((count, width), jnp.bfloat16)] * len(weights),
        compiler_params=PARAMS,
        cost_estimate=HINT,
    )(rows, *weights)


def summed_kernel(*refs):
    half = len(refs) // 2
    total = None
    for rows_ref, weight_ref in zip(refs[:half], refs[half : 2 * half]):
        part = lax.dot_general(
            rows_ref[...],
            weight_ref[...],
            (((1,), (1,)), ((), ())),
            preferred_element_type=jnp.float32,
        )
        total = part if total is None else total + part
    refs[-1][...] = total.astype(refs[-1].dtype)


def summed_products(rows, weights):
    count, depth = rows[0].shape
    height = weights[0].shape[0]
    tile = math.gcd(height, 512 if depth <= 1024 else 256)
    return pl.pallas_call(
        summed_kernel,
        grid=(height // tile,),
        in_specs=[whole(x) for x in rows]
        + [pl.BlockSpec((tile, depth), lambda i: (i, 0))] * len(weights),
        out_specs=pl.BlockSpec((count, tile), lambda i: (0, i)),
        out_shape=jax.ShapeDtypeStruct((count, height), jnp.bfloat16),
        compiler_params=PARAMS,
        cost_estimate=HINT,
    )(*rows, *weights)


class Steps:
    def __init__(self, n_ep):
        self.n_ep = n_ep
        self.held = ()

    def run(self, moves, work=None, inputs=()):
        moving = tuple(x for x, _ in moves)
        moving, inputs, self.held = lax.optimization_barrier((moving, tuple(inputs), self.held))
        arrived = [
            plane_permute(x, way, self.n_ep)
            if isinstance(way, int)
            else depth_permute(x, way, self.n_ep)
            for x, (_, way) in zip(moving, moves)
        ]
        result = () if work is None else work(*inputs)
        arrived, result = lax.optimization_barrier((arrived, result))
        self.held = (arrived, result)
        return arrived if work is None else [*arrived, result]


def to_plane(blocks):
    return [(blocks[r], r) for r in range(1, blocks.shape[0])]


def from_plane(blocks, arrived):
    return jnp.concatenate([blocks[0], *arrived], axis=0)


def tp_swap(x):
    return lax.ppermute(x, "tp", [(0, 1), (1, 0)])


def tp_sum(x):
    if lax.axis_size("tp") != 2:
        return lax.psum(x, "tp")
    return x + tp_swap(x)


def tp_reduce(x, axis):
    n_tp = lax.axis_size("tp")
    if n_tp != 2:
        return lax.psum_scatter(x, "tp", scatter_dimension=axis, tiled=True).astype(jnp.float32)
    t = lax.axis_index("tp")
    width = x.shape[axis] // 2
    mine = lax.dynamic_slice_in_dim(x, t * width, width, axis)
    other = lax.dynamic_slice_in_dim(x, (1 - t) * width, width, axis)
    return mine.astype(jnp.float32) + tp_swap(other).astype(jnp.float32)


def tp_gather(x, axis):
    n_tp = lax.axis_size("tp")
    if n_tp != 2:
        return lax.all_gather(x, "tp", axis=axis, tiled=True)
    t = lax.axis_index("tp")
    other = tp_swap(x)
    first = jnp.where(t == 0, x, other)
    second = jnp.where(t == 0, other, x)
    return jnp.concatenate([first, second], axis=axis)


def one_hot_slots(mask, capacity):
    length = mask.shape[-1]
    before = (jnp.arange(length)[:, None] < jnp.arange(length)[None, :]).astype(jnp.bfloat16)
    slots = jnp.einsum(
        "...i,ij->...j", mask.astype(jnp.bfloat16), before, preferred_element_type=jnp.float32
    )
    wanted = jnp.arange(capacity, dtype=jnp.float32)[:, None]
    return (mask[..., None, :] & (slots[..., None, :] == wanted)).astype(jnp.bfloat16)


def on_device(
    hidden_in,
    query,
    key_in,
    value_in,
    out_weight,
    norm_gain,
    router,
    routes,
    w_gate,
    w_up,
    w_down,
    grad_out,
):
    n_ep = lax.axis_size("ep")
    plane = n_ep // DEPTH
    me = lax.axis_index("ep")
    z, place = me // plane, me % plane
    n_tp, t = lax.axis_size("tp"), lax.axis_index("tp")
    length = hidden_in.shape[0]
    slice_width = hidden_in.shape[1]
    capacity = min(length, (5 * length * TOP + 4 * n_ep - 1) // (4 * n_ep))
    bf16 = jnp.bfloat16

    step = Steps(n_ep)
    steps = jnp.arange(plane, dtype=jnp.int32)
    relay_expert = z * plane + (place ^ steps)
    lanes = -(-(n_ep + TOP) // 128) * 128

    def with_lanes(x, extra):
        extra = jnp.pad(extra.astype(bf16), ((0, 0), (0, lanes - extra.shape[1])))
        return jnp.concatenate([x, extra], axis=1)

    def pack(piece, hot):
        packed = jnp.dot(hot, piece[:, :slice_width], preferred_element_type=jnp.float32)
        return packed.astype(bf16).reshape(plane, capacity, slice_width)

    def slots_of(piece, first=0):
        first += slice_width
        named = piece[:, first : first + TOP].astype(jnp.int32)
        mask = jnp.any(named[None] == relay_expert[:, None, None], axis=-1)
        return one_hot_slots(mask, capacity).reshape(plane * capacity, length)

    gate_local = w_gate[0]
    up_local = w_up[0]
    down_local = w_down[0]

    def gate_up(rows):
        return products(rows, gate_local, up_local)

    def backward_part(rows):
        return summed_products([rows], [down_local])

    score_lane = (jnp.arange(lanes) == me)[None, :]

    def expert_rows(gate_part, up_part, back_part):
        pre_sums = tp_reduce(jnp.stack([gate_part, up_part, back_part]), 2)
        gate_pre, up_pre, back = pre_sums[0], pre_sums[1], pre_sums[2]
        gate_sigmoid = jax.nn.sigmoid(gate_pre)
        gate_silu = gate_pre * gate_sigmoid
        hidden_b = lax.optimization_barrier((gate_silu * up_pre).astype(bf16)).astype(jnp.float32)
        score = tp_sum(jnp.sum(hidden_b * back, axis=1))[:, None]
        grad_gate = (back * up_pre * gate_sigmoid * (1.0 + gate_pre * (1.0 - gate_sigmoid))).astype(
            bf16
        )
        grad_up = (back * gate_silu).astype(bf16)
        both = tp_gather(jnp.stack([grad_gate, grad_up]), 2)
        expert_grad = summed_products([both[0], both[1]], [gate_local, up_local])
        rows = jnp.concatenate(
            [expert_grad, jnp.where(score_lane, score, 0.0).astype(bf16)], axis=1
        )
        return rows.reshape(plane, capacity, -1)

    def relay_sum(hot, table, arrived):
        arrived = arrived.reshape(plane * capacity, -1)
        picked_weights = jnp.take(table, relay_expert, axis=1).T[:, None, :]
        tokens = hot.reshape(plane, capacity, length)
        mix = (tokens * picked_weights).reshape(-1, length)
        total = jnp.einsum(
            "ri,rd->id", mix, arrived[:, :slice_width], preferred_element_type=jnp.float32
        )
        lane_part = jnp.einsum(
            "ri,rd->id", hot, arrived[:, slice_width:], preferred_element_type=jnp.float32
        )
        return jnp.concatenate([total, lane_part], axis=1)

    def attend(query, key_in, value_in):
        probabilities = softmax_rows(split_heads(query), split_heads(key_in))
        attended = jnp.einsum(
            "hqk,khd->qhd",
            probabilities.astype(bf16),
            split_heads(value_in),
            preferred_element_type=jnp.float32,
        )
        return probabilities, attended.reshape(length, -1).astype(bf16)

    def slots_pack(piece):
        hot = slots_of(piece)
        return hot, pack(piece, hot)

    grad_own = with_lanes(grad_out, routes)
    cols_partner, cols_near, ((probabilities, attended), (hot_own, grad_blocks)) = step.run(
        [(out_weight, SWAP), (out_weight, MIDDLE)],
        lambda *given: (attend(*given[:3]), slots_pack(given[3])),
        (query, key_in, value_in, grad_own),
    )
    query_h = split_heads(query)
    key_h = split_heads(key_in)
    value_h = split_heads(value_in)
    prob_rounded = probabilities.astype(bf16)
    cols_far, outer, *arrived = step.run(
        [(cols_partner, MIDDLE), (cols_near, OUTWARD)] + [(attended, r) for r in range(1, plane)]
    )
    cols_near = cols_near + outer
    outer, *grads, heads = step.run(
        [(cols_far, OUTWARD)] + to_plane(grad_blocks),
        lambda *parts: tp_gather(jnp.concatenate(parts, axis=0), 1),
        (attended, *arrived),
    )
    grad_rows_own = from_plane(grad_blocks, grads)
    columns = jnp.concatenate([out_weight, cols_partner, cols_near, cols_far + outer], axis=1)
    column_count = out_weight.shape[1]
    sources = jnp.stack([z, z ^ 1, jnp.where(z < 2, 2, 1), jnp.where(z < 2, 3, 0)])
    column_owner = ((place ^ steps)[:, None] + sources[None, :] * plane).reshape(n_ep)
    expert_ids = jnp.arange(n_ep, dtype=jnp.int32)
    order = jnp.argmax(column_owner[None, :] == expert_ids[:, None], axis=1)

    projected = jnp.dot(heads, columns, preferred_element_type=jnp.float32).astype(bf16)
    blocks = projected.reshape(plane, length, DEPTH * column_count)
    grad_partner, grad_near, *arrived = step.run(
        [(grad_own, SWAP), (grad_own, MIDDLE)] + [(blocks[r], r) for r in range(1, plane)]
    )
    proj = jnp.stack([blocks[0], *arrived]).reshape(plane, length, DEPTH, column_count)
    proj = proj.transpose(0, 2, 1, 3).reshape(n_ep, length, column_count)

    def normalise(proj):
        proj = proj[order].transpose(1, 0, 2).reshape(length, slice_width)
        residual = (hidden_in.astype(jnp.float32) + proj.astype(jnp.float32)).astype(bf16)
        resid_f = residual.astype(jnp.float32)
        scaled = resid_f * norm_gain.astype(jnp.float32)
        products = jnp.dot(scaled, router.astype(jnp.float32), precision=lax.Precision.HIGHEST)
        squares = jnp.sum(resid_f * resid_f, axis=1, keepdims=True)
        sums = tp_sum(jnp.concatenate([products, squares], axis=1))
        raw_logits, squares = sums[:, :n_ep], sums[:, n_ep:]
        inv_rms = lax.rsqrt(squares / D + norm_eps)
        normed = (scaled * inv_rms).astype(bf16)
        one_hot = routes[:, :, None] == expert_ids[None, None, :]
        sigmoids = jax.nn.sigmoid(raw_logits * inv_rms)
        picked = jnp.sum(jnp.where(one_hot, sigmoids[:, None, :], 0.0), axis=2)
        totals = jnp.sum(picked, axis=1, keepdims=True)
        weights = route_scale * picked / totals
        table = jnp.sum(jnp.where(one_hot, weights[:, :, None], 0.0), axis=1)
        marks = jnp.concatenate([table.astype(bf16), routes.astype(bf16)], axis=1)
        return residual, inv_rms, picked, totals, with_lanes(normed, marks)

    hot_partner, grad_blocks = slots_pack(grad_partner)
    outer, *arrived, made = step.run(
        [(grad_near, OUTWARD)] + to_plane(grad_blocks),
        normalise,
        (proj,),
    )
    residual, inv_rms, picked, totals, normed_own = made
    resid_f = residual.astype(jnp.float32)
    gain_f = norm_gain.astype(jnp.float32)
    router_f = router.astype(jnp.float32)
    one_hot = routes[:, :, None] == expert_ids[None, None, :]
    grad_rows_partner = from_plane(grad_blocks, arrived)
    grad_near = grad_near + outer

    hot_near, grad_blocks = slots_pack(grad_near)
    normed_partner, normed_near, *arrived, (back_own, back_partner, own_packed) = step.run(
        [(normed_own, SWAP), (normed_own, MIDDLE)] + to_plane(grad_blocks),
        lambda own, partner, piece, hot: (
            backward_part(own),
            backward_part(partner),
            pack(piece, hot),
        ),
        (grad_rows_own, grad_rows_partner, normed_own, hot_own),
    )
    grad_rows_near = from_plane(grad_blocks, arrived)
    blocks = pack(normed_partner, hot_partner)
    normed_far, outer, *arrived, back_near = step.run(
        [(normed_partner, MIDDLE), (normed_near, OUTWARD)] + to_plane(blocks),
        backward_part,
        (grad_rows_near,),
    )
    rows_partner = from_plane(blocks, arrived)
    normed_near = normed_near + outer
    blocks = pack(normed_near, hot_near)
    outer, grad_far, *arrived, pre_partner = step.run(
        [(normed_far, OUTWARD), (grad_partner, MIDDLE)] + to_plane(blocks),
        gate_up,
        (rows_partner,),
    )
    rows_near = from_plane(blocks, arrived)
    normed_far = normed_far + outer
    hot_far = slots_of(normed_far, n_ep)
    blocks = pack(normed_far, hot_far)
    outer, *arrived, pre_near = step.run(
        [(grad_far, OUTWARD)] + to_plane(blocks), gate_up, (rows_near,)
    )
    rows_far = from_plane(blocks, arrived)
    blocks = pack(grad_far + outer, hot_far)
    *arrived, pre_far = step.run(to_plane(blocks), gate_up, (rows_far,))
    grad_rows_far = from_plane(blocks, arrived)
    *arrived, blocks = step.run(
        to_plane(own_packed),
        lambda rows, pre: expert_rows(*pre, backward_part(rows)),
        (grad_rows_far, pre_far),
    )
    rows_own = from_plane(own_packed, arrived)

    *arrived, near_blocks = step.run(
        to_plane(blocks),
        lambda pre, back: expert_rows(*pre, back),
        (pre_near, back_near),
    )
    far_sum = relay_sum(hot_far, normed_far[:, slice_width:], from_plane(blocks, arrived))
    inward, *arrived, (partner_blocks, pre_own) = step.run(
        [(far_sum.astype(bf16), INWARD)] + to_plane(near_blocks),
        lambda pre, back, rows: (expert_rows(*pre, back), gate_up(rows)),
        (pre_partner, back_partner, rows_own),
    )
    far_sum = (far_sum + inward).astype(bf16)
    near_sum = relay_sum(hot_near, normed_near[:, slice_width:], from_plane(near_blocks, arrived))
    across, inward, *arrived, own_blocks = step.run(
        [(far_sum, MIDDLE), (near_sum.astype(bf16), INWARD)] + to_plane(partner_blocks),
        lambda pre, back: expert_rows(*pre, back),
        (pre_own, back_own),
    )
    near_sum = (near_sum + inward).astype(bf16)
    partner_sum = relay_sum(
        hot_partner, normed_partner[:, slice_width:], from_plane(partner_blocks, arrived)
    )
    partner_sum = (partner_sum + across).astype(bf16)
    near_in, partner_in, *arrived = step.run(
        [(near_sum, MIDDLE), (partner_sum, SWAP)] + to_plane(own_blocks)
    )
    own_sum = relay_sum(hot_own, normed_own[:, slice_width:], from_plane(own_blocks, arrived))
    dnormed = own_sum + near_in.astype(jnp.float32) + partner_in.astype(jnp.float32)
    ret_scores = dnormed[:, slice_width : slice_width + n_ep]
    dnormed = dnormed[:, :slice_width]
    dweight = jnp.sum(jnp.where(one_hot, ret_scores[:, None, :], 0.0), axis=2)

    dpicked = (
        route_scale / totals * (dweight - jnp.sum(dweight * picked, axis=1, keepdims=True) / totals)
    )
    dlogits = jnp.sum(
        jnp.where(one_hot, (dpicked * picked * (1.0 - picked))[:, :, None], 0.0), axis=1
    )
    dnorm_f = dnormed + jnp.dot(dlogits, router_f.T, precision=lax.Precision.HIGHEST)
    gained = gain_f * dnorm_f
    inner_sum = tp_sum(jnp.sum(gained * resid_f, axis=1))[:, None]
    dresid = inv_rms * gained - resid_f * (inv_rms * inv_rms * inv_rms) * inner_sum / D
    grad_in = (grad_out.astype(jnp.float32) + dresid).astype(bf16)
    blocks = grad_in.reshape(length, n_ep, column_count).transpose(1, 0, 2)[column_owner]
    blocks = blocks.reshape(plane, DEPTH, length, column_count).transpose(0, 2, 1, 3)
    blocks = blocks.reshape(plane, length, DEPTH * column_count)
    arrived = step.run([(blocks[r], r) for r in range(1, plane)])
    partial_heads = jnp.einsum(
        "td,hd->th",
        jnp.concatenate([blocks[0], *arrived], axis=0),
        columns,
        preferred_element_type=jnp.float32,
    )
    head_sums = tp_reduce(partial_heads.astype(bf16), 1)
    blocks = head_sums.astype(bf16).reshape(plane, length, -1)
    arrived = step.run([(blocks[r], r) for r in range(1, plane)])
    grad_attn = head_sums[:length]
    for part in arrived:
        grad_attn = grad_attn + part.astype(jnp.float32)
    grad_attn = grad_attn.astype(bf16)
    grad_h = split_heads(grad_attn)
    grad_value = jnp.einsum(
        "hqk,qhd->khd", prob_rounded, grad_h, preferred_element_type=jnp.float32
    )
    grad_prob = jnp.einsum("qhd,khd->hqk", grad_h, value_h, preferred_element_type=jnp.float32)
    centre = jnp.sum(probabilities * grad_prob, axis=2, keepdims=True)
    grad_score = (probabilities * (grad_prob - centre)).astype(bf16)
    grad_query = jnp.einsum(
        "hqk,khd->qhd", grad_score, key_h, preferred_element_type=jnp.float32
    ) * (1.0 / math.sqrt(HDIM))
    grad_key = jnp.einsum(
        "hqk,qhd->khd", grad_score, query_h, preferred_element_type=jnp.float32
    ) * (1.0 / math.sqrt(HDIM))
    return (
        grad_in,
        grad_query.reshape(length, -1).astype(bf16),
        grad_key.reshape(length, -1).astype(bf16),
        grad_value.reshape(length, -1).astype(bf16),
    )


def solution(mesh):
    in_specs = (
        P("ep", "tp"),
        P("ep", "tp"),
        P("ep", "tp"),
        P("ep", "tp"),
        P(None, ("tp", "ep")),
        P("tp"),
        P("tp", None),
        P("ep", None),
        P("ep", "tp", None),
        P("ep", "tp", None),
        P("ep", None, "tp"),
        P("ep", "tp"),
    )
    out_specs = (P("ep", "tp"), P("ep", "tp"), P("ep", "tp"), P("ep", "tp"))
    return jax.shard_map(
        on_device, mesh=mesh, in_specs=in_specs, out_specs=out_specs, check_vma=False
    )
```
